32 devices in a mesh: src: 4 (over z), xl: 8 (over y, x, core).
Axes of the slice: x: 2, y: 2, z: 4, core: 2. Of those that a mesh axis runs over, the one named last changes fastest.
Arguments:
- src_traces: float32 [64, 256, 1024], P('src', 'xl'), may hold values from -6 to 6
- rec_traces: float32 [256, 64, 1024], P('xl', 'src'), may hold values from -6 to 6
Outputs:
- multiples: float32 [64, 64, 256], P('src', 'xl')
The draws below stay inside these ranges and needn't reach their ends.
All inputs are finite; a program needn't handle non-finite values.
Results may differ from the reference program's by a relative error of at most 0.004.
Values may be sent and summed in bfloat16 or wider, within the bound.
No kernel may reach another device: no remote copies, remote signals or barrier semaphores. Data moves between devices by JAX's collectives and lax.ppermute only.
A program may use at most 64 MiB of HBM per device.

```python
import math
import jax
import jax.numpy as jnp
from jax import lax

NT = 1024
F = 128
FBASE = 4
S = 64
XPTS = 256
RCV = 64


def raised(values, stream_key, source, target, shards_of, factor):
    def block_of(axis_at):
        return (jnp.arange(values.shape[axis_at]) // (values.shape[axis_at] // shards_of)).reshape((-1,) + (1,) * (values.ndim - 1 - axis_at))

    one_side = jax.random.permutation(stream_key, shards_of)[block_of(target)]
    second = (block_of(target) + shards_of // 2) % shards_of
    return jnp.where((block_of(source) == one_side) | (block_of(source) == second), factor * values, values)


def block_scale(stream_key, shape, split, least, top_value):
    loudness, own = 1.0, jax.random.fold_in(stream_key, 6)
    for axis_at, shards_of in split:
        draws = jnp.exp(jax.random.uniform(jax.random.fold_in(own, axis_at), (shards_of,), jnp.float32, least / len(split), top_value / len(split)))
        loudness = loudness * jnp.repeat(draws, shape[axis_at] // shards_of).reshape([-1 if axis == axis_at else 1 for axis in range(len(shape))])
    return loudness


def gaussian(rng, dims, scale, reach, cuts=(), held_as=jnp.bfloat16):
    entries = scale * jax.random.normal(rng, dims, jnp.float32)
    if cuts:
        entries = entries * block_scale(rng, dims, cuts, -0.22, 0.18)
    return jnp.clip(entries, -reach, reach).astype(held_as)


def heavy_noise(stream_key, extent, scale, most, cuts, heavy, kind=jnp.bfloat16):
    array = scale * jax.random.normal(stream_key, extent, jnp.float32)
    if cuts:
        array = array * block_scale(stream_key, extent, cuts, -0.22, 0.18)
    return jnp.clip(raised(array, jax.random.fold_in(stream_key, 3), *heavy), -most, most).astype(kind)


def setup_inputs(seed: int = 0) -> dict:
    splits = jax.random.split(jax.random.key(seed), 3)
    src_traces = gaussian(splits[0], (S, XPTS, NT), 1.0, 6.0, ((0, 4), (1, 8)), jnp.float32)
    rec_traces = heavy_noise(splits[1], (XPTS, RCV, NT), 1.0, 6.0, ((0, 8), (1, 4)), (0, 1, 8, 2.0), jnp.float32)
    return dict(src_traces=src_traces, rec_traces=rec_traces)


def fourier_table(samples):
    times = jnp.arange(samples, dtype=jnp.int32)
    freq_bins = FBASE + jnp.arange(F, dtype=jnp.int32)
    phases = times[:, None] * freq_bins[None, :] % samples
    angles = phases.astype(jnp.float32) * jnp.float32(2.0 * math.pi / samples)
    basis = jnp.concatenate([jnp.cos(angles), -jnp.sin(angles)], axis=1)
    return basis / jnp.float32(math.sqrt(samples))

def spectra(traces):
    samples = traces.shape[-1]
    flat_rows = traces.reshape(-1, samples)
    result = jnp.dot(flat_rows, fourier_table(samples), precision=lax.Precision.HIGHEST, preferred_element_type=jnp.float32)
    return result.reshape(traces.shape[:-1] + (2 * F,)).astype(jnp.bfloat16)

def spectral_product(left, right):
    left_re = left[..., :F].astype(jnp.float32)
    left_im = left[..., F:].astype(jnp.float32)
    right_re = right[..., :F].astype(jnp.float32)
    right_im = right[..., F:].astype(jnp.float32)
    layout_kind = 'ltu,teu->leu'
    real_part = jnp.einsum(layout_kind, left_re, right_re) - jnp.einsum(layout_kind, left_im, right_im)
    imag_part = jnp.einsum(layout_kind, left_re, right_im) + jnp.einsum(layout_kind, left_im, right_re)
    return jnp.concatenate([real_part, imag_part], axis=-1)

def reference(src_traces, rec_traces):
    shot_source = spectra(src_traces)
    panels = spectra(rec_traces)
    return spectral_product(shot_source, panels) * jnp.float32(1.0 / math.sqrt(XPTS))
```

```python
import functools
import math

import jax
import jax.numpy as jnp
import ml_dtypes
import numpy as np
from jax import lax
from jax.experimental import pallas as pl
from jax.experimental.pallas import tpu as pltpu
from jax.sharding import PartitionSpec as P

F = 128
FBASE = 4
PIECES = 2
VMEM = 40 << 20


def fourier_table(samples):
    times = np.arange(samples)[:, None]
    phases = times * (FBASE + np.arange(F))[None, :] % samples
    angles = phases * (2.0 * math.pi / samples)
    basis = np.concatenate([np.cos(angles), -np.sin(angles)], axis=1)
    basis = (basis / math.sqrt(samples)).astype(np.float32)
    high = basis.astype(ml_dtypes.bfloat16)
    low = (basis - high.astype(np.float32)).astype(ml_dtypes.bfloat16)
    return jnp.asarray(high), jnp.asarray(low)


def spectra_kernel(traces_ref, high_ref, low_ref, out_ref):
    shape = out_ref.shape
    traces = traces_ref[...].reshape(-1, traces_ref.shape[-1])
    high = traces.astype(jnp.bfloat16)
    low = (traces - high.astype(jnp.float32)).astype(jnp.bfloat16)
    dot = functools.partial(jnp.dot, preferred_element_type=jnp.float32)
    total = dot(high, high_ref[...]) + (dot(high, low_ref[...]) + dot(low, high_ref[...]))
    out_ref[...] = total.astype(jnp.bfloat16).reshape(shape)


def spectra(traces, table, axis, piece, pieces):
    samples = traces.shape[2]
    block = list(traces.shape)
    block[axis] //= pieces
    steps = 1
    while block[0] * block[1] > 256 and block[1 - axis] % 2 == 0:
        block[1 - axis] //= 2
        steps *= 2
    out_shape = list(traces.shape[:2]) + [2 * F]
    out_shape[axis] //= pieces

    def traces_at(i):
        return (piece, i, 0) if axis == 0 else (i, piece, 0)

    def out_at(i):
        return (0, i, 0) if axis == 0 else (i, 0, 0)

    whole = pl.BlockSpec((samples, 2 * F), lambda i: (0, 0))
    rows = out_shape[0] * out_shape[1]
    return pl.pallas_call(
        spectra_kernel,
        grid=(steps,),
        in_specs=[pl.BlockSpec(tuple(block), traces_at), whole, whole],
        out_specs=pl.BlockSpec((block[0], block[1], 2 * F), out_at),
        out_shape=jax.ShapeDtypeStruct(tuple(out_shape), jnp.bfloat16),
        compiler_params=pltpu.CompilerParams(vmem_limit_bytes=VMEM),
        cost_estimate=pl.CostEstimate(
            flops=6 * rows * samples * 2 * F, bytes_accessed=4 * rows * samples, transcendentals=0
        ),
    )(traces, *table)


def split_left(ref, forms, points):
    value = ref[...].astype(jnp.float32).reshape(-1, 2 * F)
    re, im = value[:, :F], value[:, F:]
    forms[0], forms[1], forms[2] = re + im, re, im


def split_right(ref, forms):
    value = ref[...].astype(jnp.float32).reshape(-1, 2 * F)
    re, im = value[:, :F], value[:, F:]
    forms[0], forms[1], forms[2] = re, im - re, re + im


def product_tile(left, right, sources, points, width, starts, emit, start_from):
    many = 4

    def some_sources(block, carry):
        def some_points(step, sums):
            sums = list(sums)
            for inner in range(8):
                point = step * 8 + inner
                rights = [
                    [right[k, pl.ds(pl.multiple_of(point * width + at, 8), 8), :] for at in starts] for k in range(3)
                ]
                for s in range(many):
                    row = (block * many + s) * points + point
                    for k in range(3):
                        one = left[k, pl.ds(row, 1), :]
                        for g in range(len(starts)):
                            i = (s * len(starts) + g) * 3 + k
                            sums[i] = sums[i] + one * rights[k][g]
            return tuple(sums)

        zero = jnp.zeros((8, F), jnp.float32)
        sums = lax.fori_loop(0, points // 8, some_points, (zero,) * (many * len(starts) * 3))
        for s in range(many):
            for g in range(len(starts)):
                first, second, third = sums[(s * len(starts) + g) * 3 :][:3]
                emit(block * many + s, g, first - third, first + second)
        return carry

    lax.fori_loop(0, sources // many, some_sources, 0)


def tiles_kernel(core_ref, *refs, lefts, rights, tiles, carried, last):
    refs = list(refs)
    left_refs = [refs.pop(0) for _ in range(lefts)]
    right_refs = [refs.pop(0) for _ in range(rights)]
    before = refs.pop(0) if carried else None
    outs = [refs.pop(0) for _ in range(2 if last else 1)]
    left_forms, right_forms = refs
    sources, points, _ = left_refs[0].shape
    width = right_refs[0].shape[1]
    for i, ref in enumerate(left_refs):
        split_left(ref, left_forms.at[i], points)
    for i, ref in enumerate(right_refs):
        split_right(ref, right_forms.at[i])
    core = core_ref[0]
    starts = [core * 8, (1 - core) * 8]
    for tile, (left, right) in enumerate(tiles):

        def emit(source, group, re, im, tile=tile):
            if before is not None:
                re = re + before[tile, group, source, :, :F]
                im = im + before[tile, group, source, :, F:]
            if last:
                out = outs[group].at[tile, source]
                out[:, :F] = re.astype(out.dtype)
                out[:, F:] = im.astype(out.dtype)
            else:
                outs[0][tile, group, source, :, :F] = re
                outs[0][tile, group, source, :, F:] = im

        product_tile(left_forms.at[left], right_forms.at[right], sources, points, width, starts, emit, None)


def tiles_of(core, lefts, rights, tiles, before=None, last=False):
    sources, points, _ = lefts[0].shape
    width = rights[0].shape[1]
    count = len(tiles)
    if last:
        out_shape = (
            jax.ShapeDtypeStruct((count, sources, 8, 2 * F), jnp.float32),
            jax.ShapeDtypeStruct((count, sources, 8, 2 * F), jnp.bfloat16),
        )
    else:
        out_shape = jax.ShapeDtypeStruct((count, 2, sources, 8, 2 * F), jnp.float32)
    operands = list(lefts) + list(rights) + ([] if before is None else [before])
    vmem = pl.BlockSpec(memory_space=pltpu.VMEM)
    return pl.pallas_call(
        functools.partial(
            tiles_kernel, lefts=len(lefts), rights=len(rights), tiles=tiles, carried=before is not None, last=last
        ),
        in_specs=[pl.BlockSpec(memory_space=pltpu.SMEM)] + [vmem] * len(operands),
        out_specs=(vmem, vmem) if last else vmem,
        out_shape=out_shape,
        scratch_shapes=[
            pltpu.VMEM((len(lefts), 3, sources * points, F), jnp.float32),
            pltpu.VMEM((len(rights), 3, points * width, F), jnp.float32),
        ],
        compiler_params=pltpu.CompilerParams(vmem_limit_bytes=VMEM),
        cost_estimate=pl.CostEstimate(
            flops=32 * count * sources * width * points * F, bytes_accessed=1 << 20, transcendentals=0
        ),
    )(core, *operands)


def slots_kernel(turn_ref, keep_a, keep_b, came_a, came_b, *refs):
    outs, sums = refs[:4], refs[4]
    sums[0:1] = (keep_a[...] + came_a[...].astype(jnp.float32)).astype(sums.dtype)
    sums[1:4] = (keep_b[...] + came_b[...].astype(jnp.float32)).astype(sums.dtype)
    for t, out in enumerate(outs):
        out[...] = sums[turn_ref[0] ^ t]


def slots_of(turn, keep_a, keep_b, came_a, came_b):
    shape = keep_a.shape[1:]
    vmem = pl.BlockSpec(memory_space=pltpu.VMEM)
    return pl.pallas_call(
        slots_kernel,
        in_specs=[pl.BlockSpec(memory_space=pltpu.SMEM)] + [vmem] * 4,
        out_specs=(vmem,) * 4,
        out_shape=(jax.ShapeDtypeStruct(shape, jnp.bfloat16),) * 4,
        scratch_shapes=[pltpu.VMEM((4,) + shape, jnp.bfloat16)],
        compiler_params=pltpu.CompilerParams(vmem_limit_bytes=VMEM),
    )(turn, keep_a, keep_b, came_a, came_b)


def block_kernel(left_ref, right_ref, out_ref, left_forms, right_forms):
    sources, points, _ = left_ref.shape

    @pl.when(pl.program_id(0) == 0)
    def _():
        split_left(left_ref, left_forms, points)

    split_right(right_ref, right_forms)

    def emit(source, group, re, im):
        out_ref[source, :, :F] = re
        out_ref[source, :, F:] = im

    product_tile(left_forms, right_forms, sources, points, 8, [0], emit, None)


def blocks_of(left, right):
    sources, points, _ = left.shape
    receivers = right.shape[1]
    return pl.pallas_call(
        block_kernel,
        grid=(receivers // 8,),
        in_specs=[
            pl.BlockSpec((sources, points, 2 * F), lambda i: (0, 0, 0)),
            pl.BlockSpec((points, 8, 2 * F), lambda i: (0, i, 0)),
        ],
        out_specs=pl.BlockSpec((sources, 8, 2 * F), lambda i: (0, i, 0)),
        out_shape=jax.ShapeDtypeStruct((sources, receivers, 2 * F), jnp.float32),
        scratch_shapes=[
            pltpu.VMEM((3, sources * points, F), jnp.float32),
            pltpu.VMEM((3, points * 8, F), jnp.float32),
        ],
        compiler_params=pltpu.CompilerParams(vmem_limit_bytes=VMEM),
    )(left, right)


def gather_and_scatter(src_traces, rec_traces, weight):
    table = fourier_table(src_traces.shape[2])
    left = spectra(src_traces, table, 1, 0, 1)
    right = lax.all_gather(spectra(rec_traces, table, 0, 0, 1), "src", axis=1, tiled=True)
    return lax.psum_scatter(blocks_of(left, right), "xl", scatter_dimension=1, tiled=True) * weight


def swap(value, axis, flip):
    count = lax.axis_size(axis)
    return lax.ppermute(value, axis, [(i, i ^ flip) for i in range(count)])


def deliver(value, t):
    members = lax.axis_size("xl")
    pairs = []
    for z in range(lax.axis_size("src")):
        for chip in range(members // 2):
            tile = z ^ chip ^ t
            for core in range(2):
                target = (z ^ (tile & 1)) * members + (z ^ (tile & 2)) * 2 + core
                pairs.append((z * members + chip * 2 + core, target))
    return lax.ppermute(value, ("src", "xl"), pairs)


def four_planes(src_traces, rec_traces, weight):
    table = fourier_table(src_traces.shape[2])
    z, member = lax.axis_index("src"), lax.axis_index("xl")
    core = (member % 2).reshape(1).astype(jnp.int32)
    turn = (z ^ (member // 2)).reshape(1).astype(jnp.int32)
    left, right, left_far, right_far = [], [], [], []
    for piece in range(PIECES):
        right.append(spectra(rec_traces, table, 0, piece, PIECES))
        right_far.append(swap(right[-1], "src", 2))
        left.append(spectra(src_traces, table, 1, piece, PIECES))
        left_far.append(swap(left[-1], "src", 1))
    sums = None
    for piece in range(PIECES):
        sums = tiles_of(core, [left[piece]], [right[piece]], [(0, 0)], sums, piece == PIECES - 1)
    keep_a, send_a = sums
    came_a = swap(send_a, "xl", 1)
    sums = None
    for piece in range(PIECES):
        sums = tiles_of(
            core,
            [left[piece], left_far[piece]],
            [right[piece], right_far[piece]],
            [(1, 0), (0, 1), (1, 1)],
            sums,
            piece == PIECES - 1,
        )
    keep_b, send_b = sums
    came_b = swap(send_b, "xl", 1)
    slots = slots_of(turn, keep_a, keep_b, came_a, came_b)
    total = None
    for t in (2, 3, 0, 1):
        part = deliver(slots[t], t).astype(jnp.float32)
        total = part if total is None else total + part
    return total * weight


def per_device(src_traces, rec_traces):
    planes, members = lax.axis_size("src"), lax.axis_size("xl")
    weight = jnp.float32(1.0 / math.sqrt(src_traces.shape[1] * members))
    if planes == 4 and members == 8 and rec_traces.shape[1] == 16:
        return four_planes(src_traces, rec_traces, weight)
    return gather_and_scatter(src_traces, rec_traces, weight)


def solution(mesh):
    return jax.shard_map(
        per_device,
        mesh=mesh,
        in_specs=(P("src", "xl", None), P("xl", "src", None)),
        out_specs=P("src", "xl", None),
        check_vma=False,
    )
```

```python
import functools
import math

import jax
import jax.numpy as jnp
import ml_dtypes
import numpy as np
from jax import lax
from jax.experimental import pallas as pl
from jax.experimental.pallas import tpu as pltpu
from jax.sharding import PartitionSpec as P

F = 128
FBASE = 4
LEFTS = (16, 16)
RIGHTS = (16, 16)
VMEM = 40 << 20


def fourier_table(samples):
    times = np.arange(samples)[:, None]
    phases = times * (FBASE + np.arange(F))[None, :] % samples
    angles = phases * (2.0 * math.pi / samples)
    basis = np.concatenate([np.cos(angles), -np.sin(angles)], axis=1)
    basis = (basis / math.sqrt(samples)).astype(np.float32)
    high = basis.astype(ml_dtypes.bfloat16)
    low = (basis - high.astype(np.float32)).astype(ml_dtypes.bfloat16)
    return jnp.asarray(high), jnp.asarray(low)


def transform(traces, high_table, low_table):
    high = traces.astype(jnp.bfloat16)
    low = (traces - high.astype(jnp.float32)).astype(jnp.bfloat16)
    dot = functools.partial(jnp.dot, preferred_element_type=jnp.float32)
    return dot(high, high_table) + (dot(high, low_table) + dot(low, high_table))


def spectra_kernel(traces_ref, high_ref, low_ref, *refs):
    out_ref = refs[-1]
    traces = traces_ref[...].reshape(-1, traces_ref.shape[-1])
    total = transform(traces, high_ref[...], low_ref[...])
    out_ref[...] = total.astype(jnp.bfloat16).reshape(out_ref.shape)


def spectra(traces, table, axis, first, count, after=()):
    samples = traces.shape[2]
    points = 16 if first % 16 == 0 and count % 16 == 0 else 8
    block = list(traces.shape)
    block[axis] = points
    out_shape = list(traces.shape[:2]) + [2 * F]
    out_shape[axis] = count

    def at(start):
        return lambda i: (start + i, 0, 0) if axis == 0 else (0, start + i, 0)

    whole = pl.BlockSpec((samples, 2 * F), lambda i: (0, 0))
    rows = out_shape[0] * out_shape[1]
    return pl.pallas_call(
        spectra_kernel,
        grid=(count // points,),
        in_specs=[pl.BlockSpec(tuple(block), at(first // points)), whole, whole]
        + [pl.BlockSpec(memory_space=pl.ANY)] * len(after),
        out_specs=pl.BlockSpec((block[0], block[1], 2 * F), at(0)),
        out_shape=jax.ShapeDtypeStruct(tuple(out_shape), jnp.bfloat16),
        compiler_params=pltpu.CompilerParams(vmem_limit_bytes=VMEM),
        cost_estimate=pl.CostEstimate(
            flops=6 * rows * samples * 2 * F, bytes_accessed=4 * rows * samples, transcendentals=0
        ),
    )(traces, *table, *after)


def first_spectra_kernel(traces_ref, high_ref, low_ref, out_ref, traces, high, low, sems, *, steps):
    count = out_ref.shape[0]
    depth = traces.shape[2] // steps
    copies = []
    for step in range(steps):
        part = pl.ds(step * depth, depth)
        copies.append(
            [
                pltpu.make_async_copy(
                    traces_ref.at[pl.ds(0, count), :, part], traces.at[:, :, part], sems.at[step, 0]
                ),
                pltpu.make_async_copy(high_ref.at[part], high.at[part], sems.at[step, 1]),
                pltpu.make_async_copy(low_ref.at[part], low.at[part], sems.at[step, 2]),
            ]
        )
    for group in copies:
        for copy in group:
            copy.start()
    total = None
    for step, group in enumerate(copies):
        for copy in group:
            copy.wait()
        part = pl.ds(step * depth, depth)
        value = traces[:, :, part].reshape(-1, depth)
        term = transform(value, high[part], low[part])
        total = term if total is None else total + term
    out_ref[...] = total.astype(jnp.bfloat16).reshape(out_ref.shape)


def first_spectra(traces, table, count, steps=1):
    samples = traces.shape[2]
    operands = [pltpu.with_memory_space_constraint(one, pltpu.HBM) for one in (traces, *table)]
    return pl.pallas_call(
        functools.partial(first_spectra_kernel, steps=steps),
        in_specs=[pl.BlockSpec(memory_space=pltpu.HBM)] * 3,
        out_specs=pl.BlockSpec(memory_space=pltpu.VMEM),
        out_shape=jax.ShapeDtypeStruct((count, traces.shape[1], 2 * F), jnp.bfloat16),
        scratch_shapes=[
            pltpu.VMEM((count,) + traces.shape[1:], jnp.float32),
            pltpu.VMEM((samples, 2 * F), jnp.bfloat16),
            pltpu.VMEM((samples, 2 * F), jnp.bfloat16),
            pltpu.SemaphoreType.DMA((steps, 3)),
        ],
        compiler_params=pltpu.CompilerParams(vmem_limit_bytes=VMEM),
    )(*operands)


def split_left(ref, forms, first=0, count=None):
    value = ref[...] if count is None else ref[:, first : first + count]
    value = value.astype(jnp.float32).reshape(-1, 2 * F)
    re, im = value[:, :F], value[:, F:]
    forms[0], forms[1], forms[2] = re + im, re, im


def split_right(ref, forms):
    value = ref[...].astype(jnp.float32).reshape(-1, 2 * F)
    re, im = value[:, :F], value[:, F:]
    forms[0], forms[1], forms[2] = re, im - re, re + im


def product_tile(terms, sources, width, starts, emit):
    many = 4

    def some_sources(block, carry):
        zero = jnp.zeros((8, F), jnp.float32)
        sums = (zero,) * (many * len(starts) * 3)
        for left, length, first, right, points in terms:

            def some_points(step, sums, left=left, length=length, first=first, right=right):
                sums = list(sums)
                for inner in range(8):
                    point = step * 8 + inner
                    rights = [
                        [right[k, pl.ds(pl.multiple_of(point * width + at, 8), 8), :] for at in starts]
                        for k in range(3)
                    ]
                    for s in range(many):
                        row = (block * many + s) * length + first + point
                        for k in range(3):
                            one = left[k, pl.ds(row, 1), :]
                            for g in range(len(starts)):
                                i = (s * len(starts) + g) * 3 + k
                                sums[i] = sums[i] + one * rights[k][g]
                return tuple(sums)

            sums = lax.fori_loop(0, points // 8, some_points, sums)
        for s in range(many):
            for g in range(len(starts)):
                first, second, third = sums[(s * len(starts) + g) * 3 :][:3]
                emit(block * many + s, g, first - third, first + second)
        return carry

    lax.fori_loop(0, sources // many, some_sources, 0)


def tiles_kernel(core_ref, *refs, lefts, rights, tiles, ranges, carried, spare, last):
    refs = list(refs)
    left_refs = [refs.pop(0) for _ in range(lefts)]
    right_refs = [refs.pop(0) for _ in range(rights)]
    before = refs.pop(0) if carried else None
    del refs[:spare]
    outs = [refs.pop(0) for _ in range(2 if last else 1)]
    left_forms, right_forms = refs[:lefts], refs[lefts:]
    sources = left_refs[0].shape[0]
    width = right_refs[0].shape[1]
    for ref, forms, (origin, total) in zip(left_refs, left_forms, ranges):
        split_left(ref, forms, origin, total)
    for ref, forms in zip(right_refs, right_forms):
        split_right(ref, forms)
    core = core_ref[0]
    starts = [core * 8, (1 - core) * 8]
    for tile, pairs in enumerate(tiles):

        def emit(source, group, re, im, tile=tile):
            if before is not None:
                re = re + before[tile, group, source, :, :F]
                im = im + before[tile, group, source, :, F:]
            if last:
                out = outs[group].at[tile, source]
                out[:, :F] = re.astype(out.dtype)
                out[:, F:] = im.astype(out.dtype)
            else:
                outs[0][tile, group, source, :, :F] = re
                outs[0][tile, group, source, :, F:] = im

        terms = [
            (left_forms[i], ranges[i][1], first - ranges[i][0], right_forms[j], right_refs[j].shape[0])
            for i, j, first in pairs
        ]
        product_tile(terms, sources, width, starts, emit)


def tiles_of(core, lefts, rights, tiles, before=None, last=False, after=()):
    sources = lefts[0].shape[0]
    width = rights[0].shape[1]
    count = len(tiles)
    if last:
        out_shape = (
            jax.ShapeDtypeStruct((count, sources, 8, 2 * F), jnp.float32),
            jax.ShapeDtypeStruct((count, sources, 8, 2 * F), jnp.bfloat16),
        )
    else:
        out_shape = jax.ShapeDtypeStruct((count, 2, sources, 8, 2 * F), jnp.float32)
    operands = list(lefts) + list(rights) + ([] if before is None else [before])
    vmem = pl.BlockSpec(memory_space=pltpu.VMEM)
    points = sum(rights[j].shape[0] for terms in tiles for _, j, _ in terms)
    ranges = []
    for one in range(len(lefts)):
        used = [(first, first + rights[j].shape[0]) for terms in tiles for i, j, first in terms if i == one]
        origin = min(first for first, _ in used)
        ranges.append((origin, max(end for _, end in used) - origin))
    return pl.pallas_call(
        functools.partial(
            tiles_kernel,
            lefts=len(lefts),
            rights=len(rights),
            tiles=tiles,
            ranges=ranges,
            carried=before is not None,
            spare=len(after),
            last=last,
        ),
        in_specs=[pl.BlockSpec(memory_space=pltpu.SMEM)]
        + [vmem] * len(operands)
        + [pl.BlockSpec(memory_space=pl.ANY)] * len(after),
        out_specs=(vmem, vmem) if last else vmem,
        out_shape=out_shape,
        scratch_shapes=[pltpu.VMEM((3, sources * total, F), jnp.float32) for _, total in ranges]
        + [pltpu.VMEM((3, right.shape[0] * width, F), jnp.float32) for right in rights],
        compiler_params=pltpu.CompilerParams(vmem_limit_bytes=VMEM),
        cost_estimate=pl.CostEstimate(
            flops=32 * sources * width * points * F, bytes_accessed=1 << 20, transcendentals=0
        ),
    )(core, *operands, *after)


def slots_kernel(turn_ref, *refs):
    parts = (len(refs) - 5) // 2
    keep, came, outs, sums = refs[:parts], refs[parts : 2 * parts], refs[-5:-1], refs[-1]
    first = 0
    for own, other in zip(keep, came):
        count = own.shape[0]
        sums[first : first + count] = (own[...] + other[...].astype(jnp.float32)).astype(sums.dtype)
        first += count
    for t, out in enumerate(outs):
        out[...] = sums[turn_ref[0] ^ t]


def slots_of(turn, keep, came):
    shape = keep[0].shape[1:]
    vmem = pl.BlockSpec(memory_space=pltpu.VMEM)
    return pl.pallas_call(
        slots_kernel,
        in_specs=[pl.BlockSpec(memory_space=pltpu.SMEM)] + [vmem] * (2 * len(keep)),
        out_specs=(vmem,) * 4,
        out_shape=(jax.ShapeDtypeStruct(shape, jnp.bfloat16),) * 4,
        scratch_shapes=[pltpu.VMEM((4,) + shape, jnp.bfloat16)],
        compiler_params=pltpu.CompilerParams(vmem_limit_bytes=VMEM),
    )(turn, *keep, *came)


def block_kernel(left_ref, right_ref, out_ref, left_forms, right_forms):
    sources, points, _ = left_ref.shape

    @pl.when(pl.program_id(0) == 0)
    def _():
        split_left(left_ref, left_forms)

    split_right(right_ref, right_forms)

    def emit(source, group, re, im):
        out_ref[source, :, :F] = re
        out_ref[source, :, F:] = im

    product_tile([(left_forms, points, 0, right_forms, points)], sources, 8, [0], emit)


def blocks_of(left, right):
    sources, points, _ = left.shape
    receivers = right.shape[1]
    return pl.pallas_call(
        block_kernel,
        grid=(receivers // 8,),
        in_specs=[
            pl.BlockSpec((sources, points, 2 * F), lambda i: (0, 0, 0)),
            pl.BlockSpec((points, 8, 2 * F), lambda i: (0, i, 0)),
        ],
        out_specs=pl.BlockSpec((sources, 8, 2 * F), lambda i: (0, i, 0)),
        out_shape=jax.ShapeDtypeStruct((sources, receivers, 2 * F), jnp.float32),
        scratch_shapes=[
            pltpu.VMEM((3, sources * points, F), jnp.float32),
            pltpu.VMEM((3, points * 8, F), jnp.float32),
        ],
        compiler_params=pltpu.CompilerParams(vmem_limit_bytes=VMEM),
    )(left, right)


def gather_and_scatter(src_traces, rec_traces, weight):
    table = fourier_table(src_traces.shape[2])
    left = spectra(src_traces, table, 1, 0, src_traces.shape[1])
    right = lax.all_gather(spectra(rec_traces, table, 0, 0, rec_traces.shape[0]), "src", axis=1, tiled=True)
    return lax.psum_scatter(blocks_of(left, right), "xl", scatter_dimension=1, tiled=True) * weight


def swap(value, axis, flip):
    count = lax.axis_size(axis)
    return lax.ppermute(value, axis, [(i, i ^ flip) for i in range(count)])


def deliver(value, t):
    members = lax.axis_size("xl")
    pairs = []
    for z in range(lax.axis_size("src")):
        for chip in range(members // 2):
            tile = z ^ chip ^ t
            for core in range(2):
                target = (z ^ (tile & 1)) * members + (z ^ (tile & 2)) * 2 + core
                pairs.append((z * members + chip * 2 + core, target))
    return lax.ppermute(value, ("src", "xl"), pairs)


def four_planes(src_traces, rec_traces, weight):
    table = fourier_table(src_traces.shape[2])
    z, member = lax.axis_index("src"), lax.axis_index("xl")
    core = (member % 2).reshape(1).astype(jnp.int32)
    turn = (z ^ (member // 2)).reshape(1).astype(jnp.int32)
    right = [first_spectra(rec_traces, table, RIGHTS[0])]
    right_far = [swap(right[0], "src", 2)]
    left, left_far = [], []
    token = right[0]
    jobs = [("left", i, count) for i, count in enumerate(LEFTS)]
    jobs[1:1] = [("right", i, count) for i, count in enumerate(RIGHTS) if i]
    for side, i, count in jobs:
        sizes = LEFTS if side == "left" else RIGHTS
        token = spectra(
            src_traces if side == "left" else rec_traces,
            table,
            1 if side == "left" else 0,
            sum(sizes[:i]),
            count,
            (token,),
        )
        if side == "left":
            left.append(token)
            left_far.append(swap(token, "src", 1))
        else:
            right.append(token)
            right_far.append(swap(token, "src", 2))
    keep, send, came = [None] * 3, [None] * 3, [None] * 3
    others = range(1, len(RIGHTS))
    offsets = [sum(RIGHTS[:i]) - LEFTS[0] for i in range(len(RIGHTS))]
    all_here = [(0, 0, 0)] + [(1, i, offsets[i]) for i in others]
    keep[0], send[0] = tiles_of(core, left, right, [all_here], last=True, after=(token,))
    came[0] = swap(send[0], "xl", 1)
    part = tiles_of(core, left_far[:1], right[:1], [[(0, 0, 0)]], after=(keep[0],))
    sums = tiles_of(core, [left[0], left_far[0]], right_far[:1], [[(0, 0, 0)], [(1, 0, 0)]], after=(part, came[0]))
    keep[1], send[1] = tiles_of(core, left_far[1:], right[1:], [[(0, i - 1, offsets[i]) for i in others]], part, last=True, after=(sums,))
    came[1] = swap(send[1], "xl", 1)
    after = keep[1]
    for i in others:
        done = i == len(RIGHTS) - 1
        there = [[(side, 0, offsets[i])] for side in range(2)]
        sums = tiles_of(core, [left[1], left_far[1]], right_far[i : i + 1], there, sums, done, (after,))
        after = came[1]
    keep[2], send[2] = sums
    came[2] = swap(send[2], "xl", 1)
    slots = slots_of(turn, keep, came)
    total = None
    for t in (2, 3, 0, 1):
        part = deliver(slots[t], t).astype(jnp.float32)
        total = part if total is None else total + part
    return total * weight


def per_device(src_traces, rec_traces):
    planes, members = lax.axis_size("src"), lax.axis_size("xl")
    weight = jnp.float32(1.0 / math.sqrt(src_traces.shape[1] * members))
    if planes == 4 and members == 8 and rec_traces.shape[:2] == (sum(RIGHTS), 16):
        return four_planes(src_traces, rec_traces, weight)
    return gather_and_scatter(src_traces, rec_traces, weight)


def solution(mesh):
    return jax.shard_map(
        per_device,
        mesh=mesh,
        in_specs=(P("src", "xl", None), P("xl", "src", None)),
        out_specs=P("src", "xl", None),
        check_vma=False,
    )
```

```python
import functools
import math

import jax
import jax.numpy as jnp
import ml_dtypes
import numpy as np
from jax import lax
from jax.experimental import pallas as pl
from jax.experimental.pallas import tpu as pltpu
from jax.sharding import PartitionSpec as P

F = 128
FBASE = 4
VMEM = 40 << 20
POINTS = 8
ROWS = 16 * POINTS
ONES = ((0, 2), (2, 2))
OTHERS = ((0, 2), (2, 1), (3, 1))


def fourier_table(samples):
    times = np.arange(samples // 2)[:, None]
    bins = FBASE + np.arange(F)
    angles = times * bins[None, :] % samples * (2.0 * math.pi / samples)
    basis = np.concatenate([np.cos(angles), -np.sin(angles)], axis=1)
    basis = (basis / math.sqrt(samples)).astype(np.float32)
    high = basis.astype(ml_dtypes.bfloat16)
    low = (basis - high.astype(np.float32)).astype(ml_dtypes.bfloat16)
    return jnp.asarray(high), jnp.asarray(low)


def transform(traces, high_table, low_table):
    rows, samples = traces.shape
    half = samples // 2
    halves = jnp.concatenate([traces[:, :half], traces[:, half:]], axis=0)
    high = halves.astype(jnp.bfloat16)
    low = (halves - high.astype(jnp.float32)).astype(jnp.bfloat16)
    dot = functools.partial(jnp.dot, preferred_element_type=jnp.float32)
    total = dot(high, high_table) + (dot(high, low_table) + dot(low, high_table))
    odd = (FBASE + lax.broadcasted_iota(jnp.int32, (1, 2 * F), 1)) % 2
    return total[:rows] + total[rows:] * (1 - 2 * odd).astype(jnp.float32)


def spectra_kernel(traces_ref, high_ref, low_ref, out_ref):
    traces = traces_ref[...].reshape(-1, traces_ref.shape[-1])
    total = transform(traces, high_ref[...], low_ref[...])
    out_ref[...] = total.astype(jnp.bfloat16).reshape(out_ref.shape)


def spectra(traces, table):
    rows, width, samples = traces.shape
    block = 8 if rows % 8 == 0 else rows
    whole = pl.BlockSpec((samples // 2, 2 * F), lambda i: (0, 0))
    return pl.pallas_call(
        spectra_kernel,
        grid=(rows // block,),
        in_specs=[pl.BlockSpec((block, width, samples), lambda i: (i, 0, 0)), whole, whole],
        out_specs=pl.BlockSpec((block, width, 2 * F), lambda i: (i, 0, 0)),
        out_shape=jax.ShapeDtypeStruct((rows, width, 2 * F), jnp.bfloat16),
        compiler_params=pltpu.CompilerParams(vmem_limit_bytes=VMEM),
    )(traces, *table)


def first_kernel(side_ref, src_ref, rec_ref, high_ref, low_ref, out_ref, traces, high, low, sems, *, blocks):
    tables = [
        pltpu.make_async_copy(high_ref, high, sems.at[0]),
        pltpu.make_async_copy(low_ref, low, sems.at[1]),
    ]
    choices = [
        [pltpu.make_async_copy(rec_ref.at[i], traces.at[i], sems.at[2 + i]) for i in range(blocks)],
        [pltpu.make_async_copy(src_ref.at[:, i], traces.at[i], sems.at[2 + i]) for i in range(blocks)],
    ]
    for side, copies in enumerate(choices):

        @pl.when(side_ref[0] == side)
        def _(copies=copies):
            for copy in copies:
                copy.start()

    for copy in tables:
        copy.start()
    for side, copies in enumerate(choices):

        @pl.when(side_ref[0] == side)
        def _(copies=copies):
            for copy in copies:
                copy.wait()

    for copy in tables:
        copy.wait()
    total = transform(traces[...].reshape(-1, traces.shape[-1]), high[...], low[...])
    out_ref[...] = total.astype(jnp.bfloat16)


def first_spectra(side, blocks, src_blocks, rec_blocks, table):
    samples = src_blocks.shape[3]
    operands = [pltpu.with_memory_space_constraint(one, pltpu.HBM) for one in (src_blocks, rec_blocks, *table)]
    return pl.pallas_call(
        functools.partial(first_kernel, blocks=blocks),
        in_specs=[pl.BlockSpec(memory_space=pltpu.SMEM)] + [pl.BlockSpec(memory_space=pltpu.HBM)] * 4,
        out_specs=pl.BlockSpec(memory_space=pltpu.VMEM),
        out_shape=jax.ShapeDtypeStruct((blocks * ROWS, 2 * F), jnp.bfloat16),
        scratch_shapes=[
            pltpu.VMEM((blocks, 16, POINTS, samples), jnp.float32),
            pltpu.VMEM((samples // 2, 2 * F), jnp.bfloat16),
            pltpu.VMEM((samples // 2, 2 * F), jnp.bfloat16),
            pltpu.SemaphoreType.DMA((2 + blocks,)),
        ],
        compiler_params=pltpu.CompilerParams(vmem_limit_bytes=VMEM),
    )(side, *operands)


def either_kernel(side_ref, src_ref, rec_ref, high_ref, low_ref, *refs, other, first, blocks):
    out_ref = refs[-1]
    samples = src_ref.shape[-1]
    from_src = (side_ref[0] ^ other) == 1
    parts = []
    for i in range(first, first + blocks):
        src, rec = src_ref[:, i].reshape(ROWS, samples), rec_ref[i].reshape(ROWS, samples)
        parts.append(jnp.where(from_src, src, rec))
    total = transform(jnp.concatenate(parts, axis=0), high_ref[...], low_ref[...])
    out_ref[...] = total.astype(jnp.bfloat16)


def either_spectra(side, other, first, blocks, src_blocks, rec_blocks, table, after):
    samples = src_blocks.shape[3]
    rows = blocks * ROWS
    vmem = pl.BlockSpec(memory_space=pltpu.VMEM)
    return pl.pallas_call(
        functools.partial(either_kernel, other=other, first=first, blocks=blocks),
        in_specs=[pl.BlockSpec(memory_space=pltpu.SMEM)] + [vmem] * 4 + [pl.BlockSpec(memory_space=pl.ANY)],
        out_specs=vmem,
        out_shape=jax.ShapeDtypeStruct((rows, 2 * F), jnp.bfloat16),
        compiler_params=pltpu.CompilerParams(vmem_limit_bytes=VMEM),
        cost_estimate=pl.CostEstimate(
            flops=rows, bytes_accessed=rows, transcendentals=0
        ),
    )(side, src_blocks, rec_blocks, *table, after)


def products(left, right, points, starts, emit):
    many, groups = 4, len(starts)

    def some_sources(block, carry):
        def some_points(step, sums):
            sums = list(sums)
            for inner in range(POINTS):
                point = step * POINTS + inner
                rights = [
                    [right[k, pl.ds(pl.multiple_of(point * 16 + at, 8), 8), :] for at in starts] for k in range(3)
                ]
                for s in range(many):
                    row = (block * many + s) * points + point
                    for k in range(3):
                        one = left[k, pl.ds(row, 1), :]
                        for g in range(groups):
                            i = (s * groups + g) * 3 + k
                            sums[i] = sums[i] + one * rights[k][g]
            return tuple(sums)

        zero = jnp.zeros((8, F), jnp.float32)
        sums = lax.fori_loop(0, points // POINTS, some_points, (zero,) * (many * groups * 3))
        for s in range(many):
            for g in range(groups):
                first, second, third = sums[(s * groups + g) * 3 :][:3]
                emit(block * many + s, g, first - third, first + second)
        return carry

    lax.fori_loop(0, 16 // many, some_sources, 0)


def split(ref, block, forms, at, points, side):
    left = side.astype(jnp.float32)
    right = 1.0 - left

    def some_rows(step, carry):
        value = ref[pl.ds(pl.multiple_of(block * ROWS + step * 16, 16), 16)].astype(jnp.float32)
        for half in range(2):
            re, im = value[half * 8 : half * 8 + 8, :F], value[half * 8 : half * 8 + 8, F:]
            row = step * 2 + half
            start = jnp.where(side == 1, row * points + at * POINTS, at * ROWS + row * 8)
            here = pl.ds(pl.multiple_of(start, 8), 8)
            forms[0, here] = re + im * left
            forms[1, here] = im * right + re * (left - right)
            forms[2, here] = im + re * right
        return carry

    lax.fori_loop(0, ROWS // 16, some_rows, 0, unroll=2)


def tiles_kernel(side_ref, *refs, arrays, ones, others, carried, spare):
    operands, out, forms = refs[:arrays], refs[-2], refs[-1]
    before = refs[arrays] if carried else None
    side = side_ref[0]
    points = len(ones) * POINTS
    for at, (array, block) in enumerate(ones):
        split(operands[array], block, forms.at[0], at, points, side)
    for tile, blocks in enumerate(others):
        for at, (array, block) in enumerate(blocks):
            split(operands[array], block, forms.at[1 + tile], at, points, 1 - side)

    def tile_of(tile, carry):
        left = forms.at[jnp.where(side == 1, 0, 1 + tile)]
        right = forms.at[jnp.where(side == 1, 1 + tile, 0)]

        def emit(source, group, re, im):
            if carried:
                re = re + before[tile, group, source, :, :F]
                im = im + before[tile, group, source, :, F:]
            out[tile, group, source, :, :F] = re
            out[tile, group, source, :, F:] = im

        products(left, right, points, (0, 8), emit)
        return carry

    lax.fori_loop(0, len(others), tile_of, 0)


def tile_at(place, core, op):
    side, _, turn = place
    tile = turn ^ jnp.where(core == 0, 1 - op, 2 + op)
    middle = jnp.logical_or(tile == 1, tile == 2)
    return jnp.where(jnp.logical_and(middle, side == 1), 3 - tile, tile)


def with_tile(place, kept, use):
    first = 0
    for array in kept:
        count = array.shape[0]

        @pl.when(jnp.logical_and(place >= first, place < first + count))
        def _(array=array, first=first):
            use(array.at[place - first])

        first += count


def last_tiles_kernel(side_ref, core_ref, turn_ref, *refs, kept, **options):
    place = side_ref[0], core_ref[0], turn_ref[0]
    earlier, send = refs[:kept], refs[-2]
    refs = refs[kept:-2] + refs[-1:]
    tiles_kernel(side_ref, *refs, **options)
    for op in range(2):

        def use(tile, op=op):
            send[op] = tile[...].astype(send.dtype)

        with_tile(tile_at(place, 1 - place[1], op), [*earlier, refs[-2]], use)


def tiles_of(place, ones, others, before=None, after=(), kept=()):
    arrays = []

    def placed(blocks):
        result = []
        for array, block in blocks:
            if not any(array is one for one in arrays):
                arrays.append(array)
            result.append(([array is one for one in arrays].index(True), block))
        return result

    ones, others = placed(ones), [placed(blocks) for blocks in others]
    count = len(others)
    out_shape = [jax.ShapeDtypeStruct((count, 2, 16, 8, 2 * F), jnp.float32)]
    if kept:
        out_shape.append(jax.ShapeDtypeStruct((2, 2, 16, 8, 2 * F), jnp.bfloat16))
    operands = [*kept, *arrays] + ([] if before is None else [before])
    vmem = pl.BlockSpec(memory_space=pltpu.VMEM)
    options = dict(arrays=len(arrays), ones=ones, others=others, carried=before is not None, spare=len(after))
    kernel = functools.partial(tiles_kernel, **options)
    scalars = place if kept else place[:1]
    if kept:
        kernel = functools.partial(last_tiles_kernel, kept=len(kept), **options)
    result = pl.pallas_call(
        kernel,
        in_specs=[pl.BlockSpec(memory_space=pltpu.SMEM)] * len(scalars)
        + [vmem] * len(operands)
        + [pl.BlockSpec(memory_space=pl.ANY)] * len(after),
        out_specs=[vmem] * len(out_shape),
        out_shape=out_shape,
        scratch_shapes=[pltpu.VMEM((1 + count, 3, len(ones) * ROWS, F), jnp.float32)],
        compiler_params=pltpu.CompilerParams(vmem_limit_bytes=VMEM),
        cost_estimate=pl.CostEstimate(flops=count, bytes_accessed=count, transcendentals=0),
    )(*scalars, *operands, *after)
    return result if kept else result[0]


def pairs_kernel(side_ref, core_ref, turn_ref, *refs, kept):
    place = side_ref[0], core_ref[0], turn_ref[0]
    came, outs = refs[kept], refs[kept + 1 :]
    for op, out in enumerate(outs):

        def use(tile, op=op, out=out):
            out[...] = (tile[...] + came[op].astype(jnp.float32)).astype(out.dtype)

        with_tile(tile_at(place, place[1], op), refs[:kept], use)


def pairs_of(place, kept, came):
    vmem = pl.BlockSpec(memory_space=pltpu.VMEM)
    return pl.pallas_call(
        functools.partial(pairs_kernel, kept=len(kept)),
        in_specs=[pl.BlockSpec(memory_space=pltpu.SMEM)] * 3 + [vmem] * (len(kept) + 1),
        out_specs=(vmem, vmem),
        out_shape=(jax.ShapeDtypeStruct(came.shape[1:], jnp.bfloat16),) * 2,
        compiler_params=pltpu.CompilerParams(vmem_limit_bytes=VMEM),
    )(*place, *kept, came)


def halves_kernel(core_ref, first, second, keep, send):
    own = core_ref[0]
    keep[...] = first[own].astype(jnp.float32) + second[own].astype(jnp.float32)
    send[...] = (first[1 - own].astype(jnp.float32) + second[1 - own].astype(jnp.float32)).astype(send.dtype)


def halves_of(place, first, second):
    vmem = pl.BlockSpec(memory_space=pltpu.VMEM)
    return pl.pallas_call(
        halves_kernel,
        in_specs=[pl.BlockSpec(memory_space=pltpu.SMEM), vmem, vmem],
        out_specs=(vmem, vmem),
        out_shape=(
            jax.ShapeDtypeStruct(first.shape[1:], jnp.float32),
            jax.ShapeDtypeStruct(first.shape[1:], jnp.bfloat16),
        ),
        compiler_params=pltpu.CompilerParams(vmem_limit_bytes=VMEM),
    )(place[1], first, second)


def block_kernel(left_ref, right_ref, out_ref, left_forms, right_forms):
    @pl.when(pl.program_id(0) == 0)
    def _():
        value = left_ref[...].astype(jnp.float32).reshape(-1, 2 * F)
        re, im = value[:, :F], value[:, F:]
        left_forms[0], left_forms[1], left_forms[2] = re + im, re, im

    value = right_ref[...].astype(jnp.float32).reshape(-1, 2 * F)
    re, im = value[:, :F], value[:, F:]
    right_forms[0], right_forms[1], right_forms[2] = re, im - re, re + im
    sources, points, _ = left_ref.shape

    def one_source(source, carry):
        def one_point(point, sums):
            row = source * points + point
            here = pl.ds(pl.multiple_of(point * 8, 8), 8)
            return tuple(total + left_forms[k, pl.ds(row, 1), :] * right_forms[k, here, :] for k, total in enumerate(sums))

        zero = jnp.zeros((8, F), jnp.float32)
        first, second, third = lax.fori_loop(0, points, one_point, (zero,) * 3)
        out_ref[source, :, :F] = first - third
        out_ref[source, :, F:] = first + second
        return carry

    lax.fori_loop(0, sources, one_source, 0)


def blocks_of(left, right):
    sources, points, _ = left.shape
    receivers = right.shape[1]
    return pl.pallas_call(
        block_kernel,
        grid=(receivers // 8,),
        in_specs=[
            pl.BlockSpec((sources, points, 2 * F), lambda i: (0, 0, 0)),
            pl.BlockSpec((points, 8, 2 * F), lambda i: (0, i, 0)),
        ],
        out_specs=pl.BlockSpec((sources, 8, 2 * F), lambda i: (0, i, 0)),
        out_shape=jax.ShapeDtypeStruct((sources, receivers, 2 * F), jnp.float32),
        scratch_shapes=[
            pltpu.VMEM((3, sources * points, F), jnp.float32),
            pltpu.VMEM((3, points * 8, F), jnp.float32),
        ],
        compiler_params=pltpu.CompilerParams(vmem_limit_bytes=VMEM),
    )(left, right)


def gather_and_scatter(src_traces, rec_traces, weight):
    table = fourier_table(src_traces.shape[2])
    left = spectra(src_traces, table)
    right = lax.all_gather(spectra(rec_traces, table), "src", axis=1, tiled=True)
    return lax.psum_scatter(blocks_of(left, right), "xl", scatter_dimension=1, tiled=True) * weight


def swap(value, axis, flip):
    count = lax.axis_size(axis)
    return lax.ppermute(value, axis, [(i, i ^ flip) for i in range(count)])


def side_of(z):
    return (z + 1) // 2 % 2


def cross(value, other):
    return lax.ppermute(value, "src", [(z, z ^ (1 if side_of(z) ^ other else 2)) for z in range(4)])


def deliver(value, op):
    members = lax.axis_size("xl")
    pairs = []
    for z in range(lax.axis_size("src")):
        for chip in range(members // 2):
            for core in range(2):
                tile = z ^ chip ^ ((2 + op) if core else (1 - op))
                target = (z ^ (tile & 1)) * members + (z ^ (tile & 2)) * 2 + core
                pairs.append((z * members + chip * 2 + core, target))
    return lax.ppermute(value, ("src", "xl"), pairs)


def four_planes(src_traces, rec_traces, weight):
    table = fourier_table(src_traces.shape[2])
    z, member = lax.axis_index("src"), lax.axis_index("xl")
    place = [one.reshape(1).astype(jnp.int32) for one in (side_of(z), member % 2, z ^ (member // 2))]
    samples = src_traces.shape[2]
    blocks = src_traces.shape[1] // POINTS
    src_blocks = src_traces.reshape(16, blocks, POINTS, samples)
    rec_blocks = rec_traces.reshape(blocks, 16, POINTS, samples)
    one, far_one, other, far_other = [], [], [], []
    token = None
    for first, count in ONES:
        if token is None:
            token = first_spectra(place[0], count, src_blocks, rec_blocks, table)
        else:
            token = either_spectra(place[0], 0, first, count, src_blocks, rec_blocks, table, token)
        far = cross(token, 0)
        one += [(token, i) for i in range(count)]
        far_one += [(far, i) for i in range(count)]
    for first, count in OTHERS:
        token = either_spectra(place[0], 1, first, count, src_blocks, rec_blocks, table, token)
        far = cross(token, 1)
        other += [(token, i) for i in range(count)]
        far_other += [(far, i) for i in range(count)]
    early = [tiles_of(place, one, [other], after=(token,))]
    sums, after = None, (early[0],)
    for first, count in ONES:
        here = slice(first, first + count)
        sums = tiles_of(place, one[here], [far_one[here]], sums, after)
        after = ()
    early.append(sums)
    sums = None
    for first, count in OTHERS:
        here = slice(first, first + count)
        kept = early if first + count == blocks else ()
        sums = tiles_of(place, far_other[here], [other[here], far_one[here]], sums, (early[1],), kept)
    sums, send = sums
    pairs = pairs_of(place, [*early, sums], swap(send, "xl", 1))
    keep, send = halves_of(place, *[deliver(part, op) for op, part in enumerate(pairs)])
    return (keep + swap(send, "xl", 1).astype(jnp.float32)) * weight


def per_device(src_traces, rec_traces):
    planes, members = lax.axis_size("src"), lax.axis_size("xl")
    weight = float(np.float32(1.0 / math.sqrt(src_traces.shape[1] * members)))
    if planes == 4 and members == 8 and rec_traces.shape[:2] == (4 * POINTS, 16) and src_traces.shape[:2] == (16, 4 * POINTS):
        return four_planes(src_traces, rec_traces, weight)
    return gather_and_scatter(src_traces, rec_traces, weight)


def solution(mesh):
    return jax.shard_map(
        per_device,
        mesh=mesh,
        in_specs=(P("src", "xl", None), P("xl", "src", None)),
        out_specs=P("src", "xl", None),
        check_vma=False,
    )
```

```python
import functools
import math

import jax
import jax.numpy as jnp
import ml_dtypes
import numpy as np
from jax import lax
from jax.experimental import pallas as pl
from jax.experimental.pallas import tpu as pltpu
from jax.sharding import PartitionSpec as P

F = 128
FBASE = 4
VMEM = 40 << 20
POINTS = 8
ROWS = 16 * POINTS
ONES = ((0, 2), (2, 2))
OTHERS = ((0, 2), (2, 1), (3, 1))


def fourier_table(samples):
    times = np.arange(samples // 2)[:, None]
    bins = FBASE + np.arange(F)
    angles = times * bins[None, :] % samples * (2.0 * math.pi / samples)
    basis = np.concatenate([np.cos(angles), -np.sin(angles)], axis=1)
    basis = (basis / math.sqrt(samples)).astype(np.float32)
    high = basis.astype(ml_dtypes.bfloat16)
    low = (basis - high.astype(np.float32)).astype(ml_dtypes.bfloat16)
    return jnp.asarray(high), jnp.asarray(low)


def transform(traces, high_table, low_table):
    rows, samples = traces.shape
    half = samples // 2
    halves = jnp.concatenate([traces[:, :half], traces[:, half:]], axis=0)
    high = halves.astype(jnp.bfloat16)
    low = (halves - high.astype(jnp.float32)).astype(jnp.bfloat16)
    dot = functools.partial(jnp.dot, preferred_element_type=jnp.float32)
    total = dot(high, high_table) + (dot(high, low_table) + dot(low, high_table))
    odd = (FBASE + lax.broadcasted_iota(jnp.int32, (1, 2 * F), 1)) % 2
    return total[:rows] + total[rows:] * (1 - 2 * odd).astype(jnp.float32)


def spectra_kernel(traces_ref, high_ref, low_ref, out_ref):
    traces = traces_ref[...].reshape(-1, traces_ref.shape[-1])
    total = transform(traces, high_ref[...], low_ref[...])
    out_ref[...] = total.astype(jnp.bfloat16).reshape(out_ref.shape)


def spectra(traces, table):
    rows, width, samples = traces.shape
    block = 8 if rows % 8 == 0 else rows
    whole = pl.BlockSpec((samples // 2, 2 * F), lambda i: (0, 0))
    return pl.pallas_call(
        spectra_kernel,
        grid=(rows // block,),
        in_specs=[pl.BlockSpec((block, width, samples), lambda i: (i, 0, 0)), whole, whole],
        out_specs=pl.BlockSpec((block, width, 2 * F), lambda i: (i, 0, 0)),
        out_shape=jax.ShapeDtypeStruct((rows, width, 2 * F), jnp.bfloat16),
        compiler_params=pltpu.CompilerParams(vmem_limit_bytes=VMEM),
    )(traces, *table)


def first_kernel(side_ref, src_ref, rec_ref, high_ref, low_ref, out_ref, traces, high, low, sems, *, blocks):
    tables = [
        pltpu.make_async_copy(high_ref, high, sems.at[0]),
        pltpu.make_async_copy(low_ref, low, sems.at[1]),
    ]
    choices = [
        [pltpu.make_async_copy(rec_ref.at[i], traces.at[i], sems.at[2 + i]) for i in range(blocks)],
        [pltpu.make_async_copy(src_ref.at[:, i], traces.at[i], sems.at[2 + i]) for i in range(blocks)],
    ]
    for side, copies in enumerate(choices):

        @pl.when(side_ref[0] == side)
        def _(copies=copies):
            for copy in copies:
                copy.start()

    for copy in tables:
        copy.start()
    for side, copies in enumerate(choices):

        @pl.when(side_ref[0] == side)
        def _(copies=copies):
            for copy in copies:
                copy.wait()

    for copy in tables:
        copy.wait()
    total = transform(traces[...].reshape(-1, traces.shape[-1]), high[...], low[...])
    out_ref[...] = total.astype(jnp.bfloat16)


def first_spectra(side, blocks, src_blocks, rec_blocks, table):
    samples = src_blocks.shape[3]
    operands = [pltpu.with_memory_space_constraint(one, pltpu.HBM) for one in (src_blocks, rec_blocks, *table)]
    return pl.pallas_call(
        functools.partial(first_kernel, blocks=blocks),
        in_specs=[pl.BlockSpec(memory_space=pltpu.SMEM)] + [pl.BlockSpec(memory_space=pltpu.HBM)] * 4,
        out_specs=pl.BlockSpec(memory_space=pltpu.VMEM),
        out_shape=jax.ShapeDtypeStruct((blocks * ROWS, 2 * F), jnp.bfloat16),
        scratch_shapes=[
            pltpu.VMEM((blocks, 16, POINTS, samples), jnp.float32),
            pltpu.VMEM((samples // 2, 2 * F), jnp.bfloat16),
            pltpu.VMEM((samples // 2, 2 * F), jnp.bfloat16),
            pltpu.SemaphoreType.DMA((2 + blocks,)),
        ],
        compiler_params=pltpu.CompilerParams(vmem_limit_bytes=VMEM),
    )(side, *operands)


def either_kernel(side_ref, src_ref, rec_ref, high_ref, low_ref, *refs, other, first, blocks):
    out_ref = refs[-1]
    samples = src_ref.shape[-1]
    from_src = (side_ref[0] ^ other) == 1
    parts = []
    for i in range(first, first + blocks):
        src, rec = src_ref[:, i].reshape(ROWS, samples), rec_ref[i].reshape(ROWS, samples)
        parts.append(jnp.where(from_src, src, rec))
    total = transform(jnp.concatenate(parts, axis=0), high_ref[...], low_ref[...])
    out_ref[...] = total.astype(jnp.bfloat16)


def either_spectra(side, other, first, blocks, src_blocks, rec_blocks, table, after):
    samples = src_blocks.shape[3]
    rows = blocks * ROWS
    vmem = pl.BlockSpec(memory_space=pltpu.VMEM)
    return pl.pallas_call(
        functools.partial(either_kernel, other=other, first=first, blocks=blocks),
        in_specs=[pl.BlockSpec(memory_space=pltpu.SMEM)] + [vmem] * 4 + [pl.BlockSpec(memory_space=pl.ANY)],
        out_specs=vmem,
        out_shape=jax.ShapeDtypeStruct((rows, 2 * F), jnp.bfloat16),
        compiler_params=pltpu.CompilerParams(vmem_limit_bytes=VMEM),
        cost_estimate=pl.CostEstimate(
            flops=rows, bytes_accessed=rows, transcendentals=0
        ),
    )(side, src_blocks, rec_blocks, *table, after)


def products(left, right, points, starts, emit):
    many, groups = 4, len(starts)

    def some_sources(block, carry):
        def some_points(step, sums):
            sums = list(sums)
            for inner in range(POINTS):
                point = step * POINTS + inner
                rights = [
                    [right[k, pl.ds(pl.multiple_of(point * 16 + at, 8), 8), :] for at in starts] for k in range(3)
                ]
                for s in range(many):
                    row = (block * many + s) * points + point
                    for k in range(3):
                        one = left[k, pl.ds(row, 1), :]
                        for g in range(groups):
                            i = (s * groups + g) * 3 + k
                            sums[i] = sums[i] + one * rights[k][g]
            return tuple(sums)

        zero = jnp.zeros((8, F), jnp.float32)
        sums = lax.fori_loop(0, points // POINTS, some_points, (zero,) * (many * groups * 3))
        for s in range(many):
            for g in range(groups):
                first, second, third = sums[(s * groups + g) * 3 :][:3]
                emit(block * many + s, g, first - third, first + second)
        return carry

    lax.fori_loop(0, 16 // many, some_sources, 0, unroll=2)


def split(ref, block, forms, at, points, side):
    left = side.astype(jnp.float32)
    right = 1.0 - left

    def some_rows(step, carry):
        value = ref[pl.ds(pl.multiple_of(block * ROWS + step * 16, 16), 16)].astype(jnp.float32)
        for half in range(2):
            re, im = value[half * 8 : half * 8 + 8, :F], value[half * 8 : half * 8 + 8, F:]
            row = step * 2 + half
            start = jnp.where(side == 1, row * points + at * POINTS, at * ROWS + row * 8)
            here = pl.ds(pl.multiple_of(start, 8), 8)
            forms[0, here] = re + im * left
            forms[1, here] = im * right + re * (left - right)
            forms[2, here] = im + re * right
        return carry

    lax.fori_loop(0, ROWS // 16, some_rows, 0, unroll=8)


def tiles_kernel(side_ref, *refs, arrays, ones, others, carried, spare):
    operands, out, forms = refs[:arrays], refs[-2], refs[-1]
    before = refs[arrays] if carried else None
    side = side_ref[0]
    points = len(ones) * POINTS
    for at, (array, block) in enumerate(ones):
        split(operands[array], block, forms.at[0], at, points, side)
    for tile, blocks in enumerate(others):
        for at, (array, block) in enumerate(blocks):
            split(operands[array], block, forms.at[1 + tile], at, points, 1 - side)

    def tile_of(tile, carry):
        left = forms.at[jnp.where(side == 1, 0, 1 + tile)]
        right = forms.at[jnp.where(side == 1, 1 + tile, 0)]

        def emit(source, group, re, im):
            if carried:
                re = re + before[tile, group, source, :, :F]
                im = im + before[tile, group, source, :, F:]
            out[tile, group, source, :, :F] = re
            out[tile, group, source, :, F:] = im

        products(left, right, points, (0, 8), emit)
        return carry

    lax.fori_loop(0, len(others), tile_of, 0)


def tile_at(place, core, op):
    side, _, turn = place
    tile = turn ^ jnp.where(core == 0, 1 - op, 2 + op)
    middle = jnp.logical_or(tile == 1, tile == 2)
    return jnp.where(jnp.logical_and(middle, side == 1), 3 - tile, tile)


def with_tile(place, kept, use):
    first = 0
    for array in kept:
        count = array.shape[0]

        @pl.when(jnp.logical_and(place >= first, place < first + count))
        def _(array=array, first=first):
            use(array.at[place - first])

        first += count


def last_tiles_kernel(side_ref, core_ref, turn_ref, *refs, kept, **options):
    place = side_ref[0], core_ref[0], turn_ref[0]
    earlier, send = refs[:kept], refs[-2]
    refs = refs[kept:-2] + refs[-1:]
    tiles_kernel(side_ref, *refs, **options)
    for op in range(2):

        def use(tile, op=op):
            send[op] = tile[...].astype(send.dtype)

        with_tile(tile_at(place, 1 - place[1], op), [*earlier, refs[-2]], use)


def tiles_of(place, ones, others, before=None, after=(), kept=()):
    arrays = []

    def placed(blocks):
        result = []
        for array, block in blocks:
            if not any(array is one for one in arrays):
                arrays.append(array)
            result.append(([array is one for one in arrays].index(True), block))
        return result

    ones, others = placed(ones), [placed(blocks) for blocks in others]
    count = len(others)
    out_shape = [jax.ShapeDtypeStruct((count, 2, 16, 8, 2 * F), jnp.float32)]
    if kept:
        out_shape.append(jax.ShapeDtypeStruct((2, 2, 16, 8, 2 * F), jnp.bfloat16))
    operands = [*kept, *arrays] + ([] if before is None else [before])
    vmem = pl.BlockSpec(memory_space=pltpu.VMEM)
    options = dict(arrays=len(arrays), ones=ones, others=others, carried=before is not None, spare=len(after))
    kernel = functools.partial(tiles_kernel, **options)
    scalars = place if kept else place[:1]
    if kept:
        kernel = functools.partial(last_tiles_kernel, kept=len(kept), **options)
    result = pl.pallas_call(
        kernel,
        in_specs=[pl.BlockSpec(memory_space=pltpu.SMEM)] * len(scalars)
        + [vmem] * len(operands)
        + [pl.BlockSpec(memory_space=pl.ANY)] * len(after),
        out_specs=[vmem] * len(out_shape),
        out_shape=out_shape,
        scratch_shapes=[pltpu.VMEM((1 + count, 3, len(ones) * ROWS, F), jnp.float32)],
        compiler_params=pltpu.CompilerParams(vmem_limit_bytes=VMEM),
        cost_estimate=pl.CostEstimate(flops=count, bytes_accessed=count, transcendentals=0),
    )(*scalars, *operands, *after)
    return result if kept else result[0]


def pairs_kernel(side_ref, core_ref, turn_ref, *refs, kept):
    place = side_ref[0], core_ref[0], turn_ref[0]
    came, outs = refs[kept], refs[kept + 1 :]
    for op, out in enumerate(outs):

        def use(tile, op=op, out=out):
            out[...] = (tile[...] + came[op].astype(jnp.float32)).astype(out.dtype)

        with_tile(tile_at(place, place[1], op), refs[:kept], use)


def pairs_of(place, kept, came):
    vmem = pl.BlockSpec(memory_space=pltpu.VMEM)
    return pl.pallas_call(
        functools.partial(pairs_kernel, kept=len(kept)),
        in_specs=[pl.BlockSpec(memory_space=pltpu.SMEM)] * 3 + [vmem] * (len(kept) + 1),
        out_specs=(vmem, vmem),
        out_shape=(jax.ShapeDtypeStruct(came.shape[1:], jnp.bfloat16),) * 2,
        compiler_params=pltpu.CompilerParams(vmem_limit_bytes=VMEM),
    )(*place, *kept, came)


def halves_kernel(core_ref, first, second, keep, send):
    own = core_ref[0]
    keep[...] = first[own].astype(jnp.float32) + second[own].astype(jnp.float32)
    send[...] = (first[1 - own].astype(jnp.float32) + second[1 - own].astype(jnp.float32)).astype(send.dtype)


def halves_of(place, first, second):
    vmem = pl.BlockSpec(memory_space=pltpu.VMEM)
    return pl.pallas_call(
        halves_kernel,
        in_specs=[pl.BlockSpec(memory_space=pltpu.SMEM), vmem, vmem],
        out_specs=(vmem, vmem),
        out_shape=(
            jax.ShapeDtypeStruct(first.shape[1:], jnp.float32),
            jax.ShapeDtypeStruct(first.shape[1:], jnp.bfloat16),
        ),
        compiler_params=pltpu.CompilerParams(vmem_limit_bytes=VMEM),
    )(place[1], first, second)


def block_kernel(left_ref, right_ref, out_ref, left_forms, right_forms):
    @pl.when(pl.program_id(0) == 0)
    def _():
        value = left_ref[...].astype(jnp.float32).reshape(-1, 2 * F)
        re, im = value[:, :F], value[:, F:]
        left_forms[0], left_forms[1], left_forms[2] = re + im, re, im

    value = right_ref[...].astype(jnp.float32).reshape(-1, 2 * F)
    re, im = value[:, :F], value[:, F:]
    right_forms[0], right_forms[1], right_forms[2] = re, im - re, re + im
    sources, points, _ = left_ref.shape

    def one_source(source, carry):
        def one_point(point, sums):
            row = source * points + point
            here = pl.ds(pl.multiple_of(point * 8, 8), 8)
            return tuple(total + left_forms[k, pl.ds(row, 1), :] * right_forms[k, here, :] for k, total in enumerate(sums))

        zero = jnp.zeros((8, F), jnp.float32)
        first, second, third = lax.fori_loop(0, points, one_point, (zero,) * 3)
        out_ref[source, :, :F] = first - third
        out_ref[source, :, F:] = first + second
        return carry

    lax.fori_loop(0, sources, one_source, 0)


def blocks_of(left, right):
    sources, points, _ = left.shape
    receivers = right.shape[1]
    return pl.pallas_call(
        block_kernel,
        grid=(receivers // 8,),
        in_specs=[
            pl.BlockSpec((sources, points, 2 * F), lambda i: (0, 0, 0)),
            pl.BlockSpec((points, 8, 2 * F), lambda i: (0, i, 0)),
        ],
        out_specs=pl.BlockSpec((sources, 8, 2 * F), lambda i: (0, i, 0)),
        out_shape=jax.ShapeDtypeStruct((sources, receivers, 2 * F), jnp.float32),
        scratch_shapes=[
            pltpu.VMEM((3, sources * points, F), jnp.float32),
            pltpu.VMEM((3, points * 8, F), jnp.float32),
        ],
        compiler_params=pltpu.CompilerParams(vmem_limit_bytes=VMEM),
    )(left, right)


def gather_and_scatter(src_traces, rec_traces, weight):
    table = fourier_table(src_traces.shape[2])
    left = spectra(src_traces, table)
    right = lax.all_gather(spectra(rec_traces, table), "src", axis=1, tiled=True)
    return lax.psum_scatter(blocks_of(left, right), "xl", scatter_dimension=1, tiled=True) * weight


def swap(value, axis, flip):
    count = lax.axis_size(axis)
    return lax.ppermute(value, axis, [(i, i ^ flip) for i in range(count)])


def side_of(z):
    return (z + 1) // 2 % 2


def cross(value, other):
    return lax.ppermute(value, "src", [(z, z ^ (1 if side_of(z) ^ other else 2)) for z in range(4)])


def deliver(value, op):
    members = lax.axis_size("xl")
    pairs = []
    for z in range(lax.axis_size("src")):
        for chip in range(members // 2):
            for core in range(2):
                tile = z ^ chip ^ ((2 + op) if core else (1 - op))
                target = (z ^ (tile & 1)) * members + (z ^ (tile & 2)) * 2 + core
                pairs.append((z * members + chip * 2 + core, target))
    return lax.ppermute(value, ("src", "xl"), pairs)


def four_planes(src_traces, rec_traces, weight):
    table = fourier_table(src_traces.shape[2])
    z, member = lax.axis_index("src"), lax.axis_index("xl")
    place = [one.reshape(1).astype(jnp.int32) for one in (side_of(z), member % 2, z ^ (member // 2))]
    samples = src_traces.shape[2]
    blocks = src_traces.shape[1] // POINTS
    src_blocks = src_traces.reshape(16, blocks, POINTS, samples)
    rec_blocks = rec_traces.reshape(blocks, 16, POINTS, samples)
    one, far_one, other, far_other = [], [], [], []
    token = None
    for first, count in ONES:
        if token is None:
            token = first_spectra(place[0], count, src_blocks, rec_blocks, table)
        else:
            token = either_spectra(place[0], 0, first, count, src_blocks, rec_blocks, table, token)
        far = cross(token, 0)
        one += [(token, i) for i in range(count)]
        far_one += [(far, i) for i in range(count)]
    for first, count in OTHERS:
        token = either_spectra(place[0], 1, first, count, src_blocks, rec_blocks, table, token)
        far = cross(token, 1)
        other += [(token, i) for i in range(count)]
        far_other += [(far, i) for i in range(count)]
    early = [tiles_of(place, one, [other], after=(token,))]
    sums, after = None, (early[0],)
    for first, count in ONES:
        here = slice(first, first + count)
        sums = tiles_of(place, one[here], [far_one[here]], sums, after)
        after = ()
    early.append(sums)
    sums = None
    for first, count in OTHERS:
        here = slice(first, first + count)
        kept = early if first + count == blocks else ()
        sums = tiles_of(place, far_other[here], [other[here], far_one[here]], sums, (early[1],), kept)
    sums, send = sums
    pairs = pairs_of(place, [*early, sums], swap(send, "xl", 1))
    keep, send = halves_of(place, *[deliver(part, op) for op, part in enumerate(pairs)])
    return (keep + swap(send, "xl", 1).astype(jnp.float32)) * weight


def per_device(src_traces, rec_traces):
    planes, members = lax.axis_size("src"), lax.axis_size("xl")
    weight = float(np.float32(1.0 / math.sqrt(src_traces.shape[1] * members)))
    if planes == 4 and members == 8 and rec_traces.shape[:2] == (4 * POINTS, 16) and src_traces.shape[:2] == (16, 4 * POINTS):
        return four_planes(src_traces, rec_traces, weight)
    return gather_and_scatter(src_traces, rec_traces, weight)


def solution(mesh):
    return jax.shard_map(
        per_device,
        mesh=mesh,
        in_specs=(P("src", "xl", None), P("xl", "src", None)),
        out_specs=P("src", "xl", None),
        check_vma=False,
    )
```

```python
import functools
import math

import jax
import jax.numpy as jnp
import ml_dtypes
import numpy as np
from jax import lax
from jax.experimental import pallas as pl
from jax.experimental.pallas import tpu as pltpu
from jax.sharding import PartitionSpec as P

F = 128
FBASE = 4
VMEM = 40 << 20
POINTS = 8
ROWS = 16 * POINTS
ONES = ((0, 2), (2, 2))
OTHERS = ((0, 2), (2, 1), (3, 1))


def fourier_table(samples):
    times = np.arange(samples // 2)[:, None]
    bins = FBASE + np.arange(F)
    angles = times * bins[None, :] % samples * (2.0 * math.pi / samples)
    basis = np.concatenate([np.cos(angles), -np.sin(angles)], axis=1)
    basis = (basis / math.sqrt(samples)).astype(np.float32)
    high = basis.astype(ml_dtypes.bfloat16)
    low = (basis - high.astype(np.float32)).astype(ml_dtypes.bfloat16)
    return jnp.asarray(high), jnp.asarray(low)


def transform(traces, high_table, low_table):
    rows, samples = traces.shape
    half = samples // 2
    halves = jnp.concatenate([traces[:, :half], traces[:, half:]], axis=0)
    high = halves.astype(jnp.bfloat16)
    low = (halves - high.astype(jnp.float32)).astype(jnp.bfloat16)
    dot = functools.partial(jnp.dot, preferred_element_type=jnp.float32)
    total = dot(high, high_table) + (dot(high, low_table) + dot(low, high_table))
    odd = (FBASE + lax.broadcasted_iota(jnp.int32, (1, 2 * F), 1)) % 2
    return total[:rows] + total[rows:] * (1 - 2 * odd).astype(jnp.float32)


def spectra_kernel(traces_ref, high_ref, low_ref, out_ref):
    traces = traces_ref[...].reshape(-1, traces_ref.shape[-1])
    total = transform(traces, high_ref[...], low_ref[...])
    out_ref[...] = total.astype(jnp.bfloat16).reshape(out_ref.shape)


def spectra(traces, table):
    rows, width, samples = traces.shape
    block = 8 if rows % 8 == 0 else rows
    whole = pl.BlockSpec((samples // 2, 2 * F), lambda i: (0, 0))
    return pl.pallas_call(
        spectra_kernel,
        grid=(rows // block,),
        in_specs=[pl.BlockSpec((block, width, samples), lambda i: (i, 0, 0)), whole, whole],
        out_specs=pl.BlockSpec((block, width, 2 * F), lambda i: (i, 0, 0)),
        out_shape=jax.ShapeDtypeStruct((rows, width, 2 * F), jnp.bfloat16),
        compiler_params=pltpu.CompilerParams(vmem_limit_bytes=VMEM),
    )(traces, *table)


def first_kernel(side_ref, src_ref, rec_ref, high_ref, low_ref, out_ref, traces, high, low, sems, *, blocks):
    tables = [
        pltpu.make_async_copy(high_ref, high, sems.at[0]),
        pltpu.make_async_copy(low_ref, low, sems.at[1]),
    ]
    choices = [
        [pltpu.make_async_copy(rec_ref.at[i], traces.at[i], sems.at[2 + i]) for i in range(blocks)],
        [pltpu.make_async_copy(src_ref.at[:, i], traces.at[i], sems.at[2 + i]) for i in range(blocks)],
    ]
    for side, copies in enumerate(choices):

        @pl.when(side_ref[0] == side)
        def _(copies=copies):
            for copy in copies:
                copy.start()

    for copy in tables:
        copy.start()
    for side, copies in enumerate(choices):

        @pl.when(side_ref[0] == side)
        def _(copies=copies):
            for copy in copies:
                copy.wait()

    for copy in tables:
        copy.wait()
    total = transform(traces[...].reshape(-1, traces.shape[-1]), high[...], low[...])
    out_ref[...] = total.astype(jnp.bfloat16)


def first_spectra(side, blocks, src_blocks, rec_blocks, table):
    samples = src_blocks.shape[3]
    operands = [pltpu.with_memory_space_constraint(one, pltpu.HBM) for one in (src_blocks, rec_blocks, *table)]
    return pl.pallas_call(
        functools.partial(first_kernel, blocks=blocks),
        in_specs=[pl.BlockSpec(memory_space=pltpu.SMEM)] + [pl.BlockSpec(memory_space=pltpu.HBM)] * 4,
        out_specs=pl.BlockSpec(memory_space=pltpu.VMEM),
        out_shape=jax.ShapeDtypeStruct((blocks * ROWS, 2 * F), jnp.bfloat16),
        scratch_shapes=[
            pltpu.VMEM((blocks, 16, POINTS, samples), jnp.float32),
            pltpu.VMEM((samples // 2, 2 * F), jnp.bfloat16),
            pltpu.VMEM((samples // 2, 2 * F), jnp.bfloat16),
            pltpu.SemaphoreType.DMA((2 + blocks,)),
        ],
        compiler_params=pltpu.CompilerParams(vmem_limit_bytes=VMEM),
    )(side, *operands)


def either_kernel(side_ref, src_ref, rec_ref, high_ref, low_ref, *refs, other, first, blocks):
    out_ref = refs[-1]
    samples = src_ref.shape[-1]
    from_src = (side_ref[0] ^ other) == 1
    parts = []
    for i in range(first, first + blocks):
        src, rec = src_ref[:, i].reshape(ROWS, samples), rec_ref[i].reshape(ROWS, samples)
        parts.append(jnp.where(from_src, src, rec))
    total = transform(jnp.concatenate(parts, axis=0), high_ref[...], low_ref[...])
    out_ref[...] = total.astype(jnp.bfloat16)


def either_spectra(side, other, first, blocks, src_blocks, rec_blocks, table, after):
    samples = src_blocks.shape[3]
    rows = blocks * ROWS
    vmem = pl.BlockSpec(memory_space=pltpu.VMEM)
    return pl.pallas_call(
        functools.partial(either_kernel, other=other, first=first, blocks=blocks),
        in_specs=[pl.BlockSpec(memory_space=pltpu.SMEM)] + [vmem] * 4 + [pl.BlockSpec(memory_space=pl.ANY)],
        out_specs=vmem,
        out_shape=jax.ShapeDtypeStruct((rows, 2 * F), jnp.bfloat16),
        compiler_params=pltpu.CompilerParams(vmem_limit_bytes=VMEM),
        cost_estimate=pl.CostEstimate(
            flops=rows, bytes_accessed=rows, transcendentals=0
        ),
    )(side, src_blocks, rec_blocks, *table, after)


def products(left, right, points, starts, emit):
    many, groups = 4, len(starts)

    def some_sources(block, carry):
        def some_points(step, sums):
            sums = list(sums)
            for inner in range(POINTS):
                point = step * POINTS + inner
                rights = [
                    [right[k, pl.ds(pl.multiple_of(point * 16 + at, 8), 8), :] for at in starts] for k in range(3)
                ]
                for s in range(many):
                    row = (block * many + s) * points + point
                    for k in range(3):
                        one = left[k, pl.ds(row, 1), :]
                        for g in range(groups):
                            i = (s * groups + g) * 3 + k
                            sums[i] = sums[i] + one * rights[k][g]
            return tuple(sums)

        zero = jnp.zeros((8, F), jnp.float32)
        sums = lax.fori_loop(0, points // POINTS, some_points, (zero,) * (many * groups * 3))
        for s in range(many):
            for g in range(groups):
                first, second, third = sums[(s * groups + g) * 3 :][:3]
                emit(block * many + s, g, first - third, first + second)
        return carry

    lax.fori_loop(0, 16 // many, some_sources, 0, unroll=2)


def split(ref, block, forms, at, points, side):
    left = side.astype(jnp.float32)
    right = 1.0 - left

    def some_rows(step, carry):
        value = ref[pl.ds(pl.multiple_of(block * ROWS + step * 16, 16), 16)].astype(jnp.float32)
        for half in range(2):
            re, im = value[half * 8 : half * 8 + 8, :F], value[half * 8 : half * 8 + 8, F:]
            row = step * 2 + half
            start = jnp.where(side == 1, row * points + at * POINTS, at * ROWS + row * 8)
            here = pl.ds(pl.multiple_of(start, 8), 8)
            forms[0, here] = re + im * left
            forms[1, here] = im * right + re * (left - right)
            forms[2, here] = im + re * right
        return carry

    lax.fori_loop(0, ROWS // 16, some_rows, 0, unroll=8)


def tiles_kernel(side_ref, *refs, arrays, ones, others, carried, spare):
    operands, out, forms = refs[:arrays], refs[-2], refs[-1]
    before = refs[arrays] if carried else None
    side = side_ref[0]
    points = len(ones) * POINTS
    for at, (array, block) in enumerate(ones):
        split(operands[array], block, forms.at[0], at, points, side)
    for tile, blocks in enumerate(others):
        for at, (array, block) in enumerate(blocks):
            split(operands[array], block, forms.at[1 + tile], at, points, 1 - side)

    def tile_of(tile, carry):
        left = forms.at[jnp.where(side == 1, 0, 1 + tile)]
        right = forms.at[jnp.where(side == 1, 1 + tile, 0)]

        def emit(source, group, re, im):
            if carried:
                re = re + before[tile, group, source, :, :F]
                im = im + before[tile, group, source, :, F:]
            out[tile, group, source, :, :F] = re
            out[tile, group, source, :, F:] = im

        products(left, right, points, (0, 8), emit)
        return carry

    lax.fori_loop(0, len(others), tile_of, 0)


def tile_at(place, core, op):
    side, _, turn = place
    tile = turn ^ jnp.where(core == 0, 1 - op, 2 + op)
    middle = jnp.logical_or(tile == 1, tile == 2)
    return jnp.where(jnp.logical_and(middle, side == 1), 3 - tile, tile)


def with_tile(place, kept, use):
    first = 0
    for array in kept:
        count = array.shape[0]

        @pl.when(jnp.logical_and(place >= first, place < first + count))
        def _(array=array, first=first):
            use(array.at[place - first])

        first += count


def last_tiles_kernel(side_ref, core_ref, turn_ref, *refs, kept, **options):
    place = side_ref[0], core_ref[0], turn_ref[0]
    earlier, send = refs[:kept], refs[-2]
    refs = refs[kept:-2] + refs[-1:]
    tiles_kernel(side_ref, *refs, **options)
    for op in range(2):

        def use(tile, op=op):
            send[op] = tile[...].astype(send.dtype)

        with_tile(tile_at(place, 1 - place[1], op), [*earlier, refs[-2]], use)


def tiles_of(place, ones, others, before=None, after=(), kept=()):
    arrays = []

    def placed(blocks):
        result = []
        for array, block in blocks:
            if not any(array is one for one in arrays):
                arrays.append(array)
            result.append(([array is one for one in arrays].index(True), block))
        return result

    ones, others = placed(ones), [placed(blocks) for blocks in others]
    count = len(others)
    out_shape = [jax.ShapeDtypeStruct((count, 2, 16, 8, 2 * F), jnp.float32)]
    if kept:
        out_shape.append(jax.ShapeDtypeStruct((2, 2, 16, 8, 2 * F), jnp.bfloat16))
    operands = [*kept, *arrays] + ([] if before is None else [before])
    vmem = pl.BlockSpec(memory_space=pltpu.VMEM)
    options = dict(arrays=len(arrays), ones=ones, others=others, carried=before is not None, spare=len(after))
    kernel = functools.partial(tiles_kernel, **options)
    scalars = place if kept else place[:1]
    if kept:
        kernel = functools.partial(last_tiles_kernel, kept=len(kept), **options)
    result = pl.pallas_call(
        kernel,
        in_specs=[pl.BlockSpec(memory_space=pltpu.SMEM)] * len(scalars)
        + [vmem] * len(operands)
        + [pl.BlockSpec(memory_space=pl.ANY)] * len(after),
        out_specs=[vmem] * len(out_shape),
        out_shape=out_shape,
        scratch_shapes=[pltpu.VMEM((1 + count, 3, len(ones) * ROWS, F), jnp.float32)],
        compiler_params=pltpu.CompilerParams(vmem_limit_bytes=VMEM),
        cost_estimate=pl.CostEstimate(flops=count, bytes_accessed=count, transcendentals=0),
    )(*scalars, *operands, *after)
    return result if kept else result[0]


def pairs_kernel(side_ref, core_ref, turn_ref, *refs, kept):
    place = side_ref[0], core_ref[0], turn_ref[0]
    came, first, second, third = refs[kept:]

    def use_first(tile):
        first[...] = (tile[...] + came[0].astype(jnp.float32)).astype(first.dtype)

    def use_second(tile):
        for out, half in ((second, place[1]), (third, 1 - place[1])):
            out[...] = (tile[half] + came[1, half].astype(jnp.float32)).astype(out.dtype)

    for op, use in enumerate((use_first, use_second)):
        with_tile(tile_at(place, place[1], op), refs[:kept], use)


def pairs_of(place, kept, came):
    vmem = pl.BlockSpec(memory_space=pltpu.VMEM)
    shape = came.shape[1:]
    return pl.pallas_call(
        functools.partial(pairs_kernel, kept=len(kept)),
        in_specs=[pl.BlockSpec(memory_space=pltpu.SMEM)] * 3 + [vmem] * (len(kept) + 1),
        out_specs=(vmem,) * 3,
        out_shape=[jax.ShapeDtypeStruct(one, jnp.bfloat16) for one in (shape, shape[1:], shape[1:])],
        compiler_params=pltpu.CompilerParams(vmem_limit_bytes=VMEM),
    )(*place, *kept, came)


def halves_kernel(core_ref, whole, keep, send):
    own = core_ref[0]
    keep[...] = whole[own]
    send[...] = whole[1 - own]


def halves_of(place, whole):
    vmem = pl.BlockSpec(memory_space=pltpu.VMEM)
    return pl.pallas_call(
        halves_kernel,
        in_specs=[pl.BlockSpec(memory_space=pltpu.SMEM), vmem],
        out_specs=(vmem, vmem),
        out_shape=(jax.ShapeDtypeStruct(whole.shape[1:], jnp.bfloat16),) * 2,
        compiler_params=pltpu.CompilerParams(vmem_limit_bytes=VMEM),
    )(place[1], whole)


def block_kernel(left_ref, right_ref, out_ref, left_forms, right_forms):
    @pl.when(pl.program_id(0) == 0)
    def _():
        value = left_ref[...].astype(jnp.float32).reshape(-1, 2 * F)
        re, im = value[:, :F], value[:, F:]
        left_forms[0], left_forms[1], left_forms[2] = re + im, re, im

    value = right_ref[...].astype(jnp.float32).reshape(-1, 2 * F)
    re, im = value[:, :F], value[:, F:]
    right_forms[0], right_forms[1], right_forms[2] = re, im - re, re + im
    sources, points, _ = left_ref.shape

    def one_source(source, carry):
        def one_point(point, sums):
            row = source * points + point
            here = pl.ds(pl.multiple_of(point * 8, 8), 8)
            return tuple(total + left_forms[k, pl.ds(row, 1), :] * right_forms[k, here, :] for k, total in enumerate(sums))

        zero = jnp.zeros((8, F), jnp.float32)
        first, second, third = lax.fori_loop(0, points, one_point, (zero,) * 3)
        out_ref[source, :, :F] = first - third
        out_ref[source, :, F:] = first + second
        return carry

    lax.fori_loop(0, sources, one_source, 0)


def blocks_of(left, right):
    sources, points, _ = left.shape
    receivers = right.shape[1]
    return pl.pallas_call(
        block_kernel,
        grid=(receivers // 8,),
        in_specs=[
            pl.BlockSpec((sources, points, 2 * F), lambda i: (0, 0, 0)),
            pl.BlockSpec((points, 8, 2 * F), lambda i: (0, i, 0)),
        ],
        out_specs=pl.BlockSpec((sources, 8, 2 * F), lambda i: (0, i, 0)),
        out_shape=jax.ShapeDtypeStruct((sources, receivers, 2 * F), jnp.float32),
        scratch_shapes=[
            pltpu.VMEM((3, sources * points, F), jnp.float32),
            pltpu.VMEM((3, points * 8, F), jnp.float32),
        ],
        compiler_params=pltpu.CompilerParams(vmem_limit_bytes=VMEM),
    )(left, right)


def gather_and_scatter(src_traces, rec_traces, weight):
    table = fourier_table(src_traces.shape[2])
    left = spectra(src_traces, table)
    right = lax.all_gather(spectra(rec_traces, table), "src", axis=1, tiled=True)
    return lax.psum_scatter(blocks_of(left, right), "xl", scatter_dimension=1, tiled=True) * weight


def swap(value, axis, flip):
    count = lax.axis_size(axis)
    return lax.ppermute(value, axis, [(i, i ^ flip) for i in range(count)])


def side_of(z):
    return (z + 1) // 2 % 2


def cross(value, other):
    return lax.ppermute(value, "src", [(z, z ^ (1 if side_of(z) ^ other else 2)) for z in range(4)])


def deliver(value, op, flip):
    members = lax.axis_size("xl")
    pairs = []
    for z in range(lax.axis_size("src")):
        for chip in range(members // 2):
            for core in range(2):
                tile = z ^ chip ^ ((2 + op) if core else (1 - op))
                target = (z ^ (tile & 1)) * members + (z ^ (tile & 2)) * 2 + (core ^ flip)
                pairs.append((z * members + chip * 2 + core, target))
    return lax.ppermute(value, ("src", "xl"), pairs)


def four_planes(src_traces, rec_traces, weight):
    table = fourier_table(src_traces.shape[2])
    z, member = lax.axis_index("src"), lax.axis_index("xl")
    place = [one.reshape(1).astype(jnp.int32) for one in (side_of(z), member % 2, z ^ (member // 2))]
    samples = src_traces.shape[2]
    blocks = src_traces.shape[1] // POINTS
    src_blocks = src_traces.reshape(16, blocks, POINTS, samples)
    rec_blocks = rec_traces.reshape(blocks, 16, POINTS, samples)
    one, far_one, other, far_other = [], [], [], []
    token = None
    for first, count in ONES:
        if token is None:
            token = first_spectra(place[0], count, src_blocks, rec_blocks, table)
        else:
            token = either_spectra(place[0], 0, first, count, src_blocks, rec_blocks, table, token)
        far = cross(token, 0)
        one += [(token, i) for i in range(count)]
        far_one += [(far, i) for i in range(count)]
    for first, count in OTHERS:
        token = either_spectra(place[0], 1, first, count, src_blocks, rec_blocks, table, token)
        far = cross(token, 1)
        other += [(token, i) for i in range(count)]
        far_other += [(far, i) for i in range(count)]
    early = [tiles_of(place, one, [other], after=(token,))]
    sums, after = None, (early[0],)
    for first, count in ONES:
        here = slice(first, first + count)
        sums = tiles_of(place, one[here], [far_one[here]], sums, after)
        after = ()
    early.append(sums)
    sums = None
    for first, count in OTHERS:
        here = slice(first, first + count)
        kept = early if first + count == blocks else ()
        sums = tiles_of(place, far_other[here], [other[here], far_one[here]], sums, (early[1],), kept)
    sums, send = sums
    first, second, third = pairs_of(place, [*early, sums], swap(send, "xl", 1))
    keep, send = halves_of(place, deliver(first, 0, 0))
    parts = [keep, swap(send, "xl", 1), deliver(second, 1, 0), deliver(third, 1, 1)]
    return sum(part.astype(jnp.float32) for part in parts) * weight


def per_device(src_traces, rec_traces):
    planes, members = lax.axis_size("src"), lax.axis_size("xl")
    weight = float(np.float32(1.0 / math.sqrt(src_traces.shape[1] * members)))
    if planes == 4 and members == 8 and rec_traces.shape[:2] == (4 * POINTS, 16) and src_traces.shape[:2] == (16, 4 * POINTS):
        return four_planes(src_traces, rec_traces, weight)
    return gather_and_scatter(src_traces, rec_traces, weight)


def solution(mesh):
    return jax.shard_map(
        per_device,
        mesh=mesh,
        in_specs=(P("src", "xl", None), P("xl", "src", None)),
        out_specs=P("src", "xl", None),
        check_vma=False,
    )
```

```python
import functools
import math

import jax
import jax.numpy as jnp
import ml_dtypes
import numpy as np
from jax import lax
from jax.experimental import pallas as pl
from jax.experimental.pallas import tpu as pltpu
from jax.sharding import PartitionSpec as P

F = 128
FBASE = 4
VMEM = 40 << 20
POINTS = 8
ROWS = 16 * POINTS
ONES = ((0, 2), (2, 2))
OTHERS = ((0, 2), (2, 1), (3, 1))
TURNS = ((3, 2), (0, 1))


def fourier_table(samples):
    times = np.arange(samples // 2)[:, None]
    bins = FBASE + np.arange(F)
    angles = times * bins[None, :] % samples * (2.0 * math.pi / samples)
    basis = np.concatenate([np.cos(angles), -np.sin(angles)], axis=1)
    basis = (basis / math.sqrt(samples)).astype(np.float32)
    high = basis.astype(ml_dtypes.bfloat16)
    low = (basis - high.astype(np.float32)).astype(ml_dtypes.bfloat16)
    return jnp.asarray(high), jnp.asarray(low)


def transform(traces, high_table, low_table):
    rows, samples = traces.shape
    half = samples // 2
    halves = jnp.concatenate([traces[:, :half], traces[:, half:]], axis=0)
    high = halves.astype(jnp.bfloat16)
    low = (halves - high.astype(jnp.float32)).astype(jnp.bfloat16)
    dot = functools.partial(jnp.dot, preferred_element_type=jnp.float32)
    total = dot(high, high_table) + (dot(high, low_table) + dot(low, high_table))
    odd = (FBASE + lax.broadcasted_iota(jnp.int32, (1, 2 * F), 1)) % 2
    return total[:rows] + total[rows:] * (1 - 2 * odd).astype(jnp.float32)


def spectra_kernel(traces_ref, high_ref, low_ref, out_ref):
    traces = traces_ref[...].reshape(-1, traces_ref.shape[-1])
    total = transform(traces, high_ref[...], low_ref[...])
    out_ref[...] = total.astype(jnp.bfloat16).reshape(out_ref.shape)


def spectra(traces, table):
    rows, width, samples = traces.shape
    block = 8 if rows % 8 == 0 else rows
    whole = pl.BlockSpec((samples // 2, 2 * F), lambda i: (0, 0))
    return pl.pallas_call(
        spectra_kernel,
        grid=(rows // block,),
        in_specs=[pl.BlockSpec((block, width, samples), lambda i: (i, 0, 0)), whole, whole],
        out_specs=pl.BlockSpec((block, width, 2 * F), lambda i: (i, 0, 0)),
        out_shape=jax.ShapeDtypeStruct((rows, width, 2 * F), jnp.bfloat16),
        compiler_params=pltpu.CompilerParams(vmem_limit_bytes=VMEM),
    )(traces, *table)


def first_kernel(side_ref, src_ref, rec_ref, high_ref, low_ref, out_ref, traces, high, low, sems, *, blocks):
    tables = [
        pltpu.make_async_copy(high_ref, high, sems.at[0]),
        pltpu.make_async_copy(low_ref, low, sems.at[1]),
    ]
    choices = [
        [pltpu.make_async_copy(rec_ref.at[i], traces.at[i], sems.at[2 + i]) for i in range(blocks)],
        [pltpu.make_async_copy(src_ref.at[:, i], traces.at[i], sems.at[2 + i]) for i in range(blocks)],
    ]
    for side, copies in enumerate(choices):

        @pl.when(side_ref[0] == side)
        def _(copies=copies):
            for copy in copies:
                copy.start()

    for copy in tables:
        copy.start()
    for side, copies in enumerate(choices):

        @pl.when(side_ref[0] == side)
        def _(copies=copies):
            for copy in copies:
                copy.wait()

    for copy in tables:
        copy.wait()
    total = transform(traces[...].reshape(-1, traces.shape[-1]), high[...], low[...])
    out_ref[...] = total.astype(jnp.bfloat16)


def first_spectra(side, blocks, src_blocks, rec_blocks, table):
    samples = src_blocks.shape[3]
    operands = [pltpu.with_memory_space_constraint(one, pltpu.HBM) for one in (src_blocks, rec_blocks, *table)]
    return pl.pallas_call(
        functools.partial(first_kernel, blocks=blocks),
        in_specs=[pl.BlockSpec(memory_space=pltpu.SMEM)] + [pl.BlockSpec(memory_space=pltpu.HBM)] * 4,
        out_specs=pl.BlockSpec(memory_space=pltpu.VMEM),
        out_shape=jax.ShapeDtypeStruct((blocks * ROWS, 2 * F), jnp.bfloat16),
        scratch_shapes=[
            pltpu.VMEM((blocks, 16, POINTS, samples), jnp.float32),
            pltpu.VMEM((samples // 2, 2 * F), jnp.bfloat16),
            pltpu.VMEM((samples // 2, 2 * F), jnp.bfloat16),
            pltpu.SemaphoreType.DMA((2 + blocks,)),
        ],
        compiler_params=pltpu.CompilerParams(vmem_limit_bytes=VMEM),
    )(side, *operands)


def either_kernel(side_ref, src_ref, rec_ref, high_ref, low_ref, *refs, other, first, blocks):
    out_ref = refs[-1]
    samples = src_ref.shape[-1]
    from_src = (side_ref[0] ^ other) == 1
    parts = []
    for i in range(first, first + blocks):
        src, rec = src_ref[:, i].reshape(ROWS, samples), rec_ref[i].reshape(ROWS, samples)
        parts.append(jnp.where(from_src, src, rec))
    total = transform(jnp.concatenate(parts, axis=0), high_ref[...], low_ref[...])
    out_ref[...] = total.astype(jnp.bfloat16)


def either_spectra(side, other, first, blocks, src_blocks, rec_blocks, table, after):
    samples = src_blocks.shape[3]
    rows = blocks * ROWS
    vmem = pl.BlockSpec(memory_space=pltpu.VMEM)
    return pl.pallas_call(
        functools.partial(either_kernel, other=other, first=first, blocks=blocks),
        in_specs=[pl.BlockSpec(memory_space=pltpu.SMEM)] + [vmem] * 4 + [pl.BlockSpec(memory_space=pl.ANY)],
        out_specs=vmem,
        out_shape=jax.ShapeDtypeStruct((rows, 2 * F), jnp.bfloat16),
        compiler_params=pltpu.CompilerParams(vmem_limit_bytes=VMEM),
        cost_estimate=pl.CostEstimate(
            flops=rows, bytes_accessed=rows, transcendentals=0
        ),
    )(side, src_blocks, rec_blocks, *table, after)


def products(left, right, points, starts, emit):
    many, groups = 4, len(starts)

    def some_sources(block, carry):
        def some_points(step, sums):
            sums = list(sums)
            for inner in range(POINTS):
                point = step * POINTS + inner
                rights = [
                    [right[k, pl.ds(pl.multiple_of(point * 16 + at, 8), 8), :] for at in starts] for k in range(3)
                ]
                for s in range(many):
                    row = (block * many + s) * points + point
                    for k in range(3):
                        one = left[k, pl.ds(row, 1), :]
                        for g in range(groups):
                            i = (s * groups + g) * 3 + k
                            sums[i] = sums[i] + one * rights[k][g]
            return tuple(sums)

        zero = jnp.zeros((8, F), jnp.float32)
        sums = lax.fori_loop(0, points // POINTS, some_points, (zero,) * (many * groups * 3))
        for s in range(many):
            for g in range(groups):
                first, second, third = sums[(s * groups + g) * 3 :][:3]
                emit(block * many + s, g, first - third, first + second)
        return carry

    lax.fori_loop(0, 16 // many, some_sources, 0, unroll=2)


def split(ref, block, forms, at, points, side):
    left = side.astype(jnp.float32)
    right = 1.0 - left

    def some_rows(step, carry):
        value = ref[pl.ds(pl.multiple_of(block * ROWS + step * 16, 16), 16)].astype(jnp.float32)
        for half in range(2):
            re, im = value[half * 8 : half * 8 + 8, :F], value[half * 8 : half * 8 + 8, F:]
            row = step * 2 + half
            start = jnp.where(side == 1, row * points + at * POINTS, at * ROWS + row * 8)
            here = pl.ds(pl.multiple_of(start, 8), 8)
            forms[0, here] = re + im * left
            forms[1, here] = im * right + re * (left - right)
            forms[2, here] = im + re * right
        return carry

    lax.fori_loop(0, ROWS // 16, some_rows, 0, unroll=8)


def tiles_kernel(side_ref, *refs, arrays, ones, others, carried, spare):
    operands, out, forms = refs[:arrays], refs[-2], refs[-1]
    before = refs[arrays] if carried else None
    side = side_ref[0]
    points = len(ones) * POINTS
    for at, (array, block) in enumerate(ones):
        split(operands[array], block, forms.at[0], at, points, side)
    for tile, blocks in enumerate(others):
        for at, (array, block) in enumerate(blocks):
            split(operands[array], block, forms.at[1 + tile], at, points, 1 - side)

    def tile_of(tile, carry):
        left = forms.at[jnp.where(side == 1, 0, 1 + tile)]
        right = forms.at[jnp.where(side == 1, 1 + tile, 0)]

        def emit(source, group, re, im):
            if carried:
                re = re + before[tile, group, source, :, :F]
                im = im + before[tile, group, source, :, F:]
            out[tile, group, source, :, :F] = re
            out[tile, group, source, :, F:] = im

        products(left, right, points, (0, 8), emit)
        return carry

    lax.fori_loop(0, len(others), tile_of, 0)


def tile_at(place, core, op):
    side, _, turn = place
    tile = turn ^ jnp.where(core == 0, *TURNS[op])
    middle = jnp.logical_or(tile == 1, tile == 2)
    return jnp.where(jnp.logical_and(middle, side == 1), 3 - tile, tile)


def with_tile(place, kept, use):
    first = 0
    for array in kept:
        count = array.shape[0]

        @pl.when(jnp.logical_and(place >= first, place < first + count))
        def _(array=array, first=first):
            use(array.at[place - first])

        first += count


def last_tiles_kernel(side_ref, core_ref, turn_ref, *refs, kept, **options):
    place = side_ref[0], core_ref[0], turn_ref[0]
    earlier, sends = refs[:kept], refs[-3:-1]
    refs = refs[kept:-3] + refs[-1:]
    tiles_kernel(side_ref, *refs, **options)
    for op, send in enumerate(sends):

        def use(tile, send=send):
            send[...] = tile[...].astype(send.dtype)

        with_tile(tile_at(place, 1 - place[1], op), [*earlier, refs[-2]], use)


def tiles_of(place, ones, others, before=None, after=(), kept=()):
    arrays = []

    def placed(blocks):
        result = []
        for array, block in blocks:
            if not any(array is one for one in arrays):
                arrays.append(array)
            result.append(([array is one for one in arrays].index(True), block))
        return result

    ones, others = placed(ones), [placed(blocks) for blocks in others]
    count = len(others)
    out_shape = [jax.ShapeDtypeStruct((count, 2, 16, 8, 2 * F), jnp.float32)]
    if kept:
        out_shape += [jax.ShapeDtypeStruct((2, 16, 8, 2 * F), jnp.bfloat16)] * 2
    operands = [*kept, *arrays] + ([] if before is None else [before])
    vmem = pl.BlockSpec(memory_space=pltpu.VMEM)
    options = dict(arrays=len(arrays), ones=ones, others=others, carried=before is not None, spare=len(after))
    kernel = functools.partial(tiles_kernel, **options)
    scalars = place if kept else place[:1]
    if kept:
        kernel = functools.partial(last_tiles_kernel, kept=len(kept), **options)
    result = pl.pallas_call(
        kernel,
        in_specs=[pl.BlockSpec(memory_space=pltpu.SMEM)] * len(scalars)
        + [vmem] * len(operands)
        + [pl.BlockSpec(memory_space=pl.ANY)] * len(after),
        out_specs=[vmem] * len(out_shape),
        out_shape=out_shape,
        scratch_shapes=[pltpu.VMEM((1 + count, 3, len(ones) * ROWS, F), jnp.float32)],
        compiler_params=pltpu.CompilerParams(vmem_limit_bytes=VMEM),
        cost_estimate=pl.CostEstimate(flops=count, bytes_accessed=count, transcendentals=0),
    )(*scalars, *operands, *after)
    return result if kept else result[0]


def first_kernel_of_pair(side_ref, core_ref, turn_ref, *refs, kept):
    place = side_ref[0], core_ref[0], turn_ref[0]
    came, out = refs[kept:]

    def use(tile):
        out[...] = (tile[...] + came[...].astype(jnp.float32)).astype(out.dtype)

    with_tile(tile_at(place, place[1], 0), refs[:kept], use)


def second_kernel_of_pair(side_ref, core_ref, turn_ref, *refs, kept):
    place = side_ref[0], core_ref[0], turn_ref[0]
    came = refs[kept]

    def use(tile):
        for out, half in zip(refs[kept + 1 :], (place[1], 1 - place[1])):
            out[...] = (tile[half] + came[half].astype(jnp.float32)).astype(out.dtype)

    with_tile(tile_at(place, place[1], 1), refs[:kept], use)


def pair_of(kernel, place, kept, came, shapes):
    vmem = pl.BlockSpec(memory_space=pltpu.VMEM)
    return pl.pallas_call(
        functools.partial(kernel, kept=len(kept)),
        in_specs=[pl.BlockSpec(memory_space=pltpu.SMEM)] * 3 + [vmem] * (len(kept) + 1),
        out_specs=[vmem] * len(shapes),
        out_shape=[jax.ShapeDtypeStruct(one, jnp.bfloat16) for one in shapes],
        compiler_params=pltpu.CompilerParams(vmem_limit_bytes=VMEM),
    )(*place, *kept, came)


def halves_kernel(core_ref, whole, keep, send):
    own = core_ref[0]
    keep[...] = whole[own]
    send[...] = whole[1 - own]


def halves_of(place, whole):
    vmem = pl.BlockSpec(memory_space=pltpu.VMEM)
    return pl.pallas_call(
        halves_kernel,
        in_specs=[pl.BlockSpec(memory_space=pltpu.SMEM), vmem],
        out_specs=(vmem, vmem),
        out_shape=(jax.ShapeDtypeStruct(whole.shape[1:], jnp.bfloat16),) * 2,
        compiler_params=pltpu.CompilerParams(vmem_limit_bytes=VMEM),
    )(place[1], whole)


def block_kernel(left_ref, right_ref, out_ref, left_forms, right_forms):
    @pl.when(pl.program_id(0) == 0)
    def _():
        value = left_ref[...].astype(jnp.float32).reshape(-1, 2 * F)
        re, im = value[:, :F], value[:, F:]
        left_forms[0], left_forms[1], left_forms[2] = re + im, re, im

    value = right_ref[...].astype(jnp.float32).reshape(-1, 2 * F)
    re, im = value[:, :F], value[:, F:]
    right_forms[0], right_forms[1], right_forms[2] = re, im - re, re + im
    sources, points, _ = left_ref.shape

    def one_source(source, carry):
        def one_point(point, sums):
            row = source * points + point
            here = pl.ds(pl.multiple_of(point * 8, 8), 8)
            return tuple(total + left_forms[k, pl.ds(row, 1), :] * right_forms[k, here, :] for k, total in enumerate(sums))

        zero = jnp.zeros((8, F), jnp.float32)
        first, second, third = lax.fori_loop(0, points, one_point, (zero,) * 3)
        out_ref[source, :, :F] = first - third
        out_ref[source, :, F:] = first + second
        return carry

    lax.fori_loop(0, sources, one_source, 0)


def blocks_of(left, right):
    sources, points, _ = left.shape
    receivers = right.shape[1]
    return pl.pallas_call(
        block_kernel,
        grid=(receivers // 8,),
        in_specs=[
            pl.BlockSpec((sources, points, 2 * F), lambda i: (0, 0, 0)),
            pl.BlockSpec((points, 8, 2 * F), lambda i: (0, i, 0)),
        ],
        out_specs=pl.BlockSpec((sources, 8, 2 * F), lambda i: (0, i, 0)),
        out_shape=jax.ShapeDtypeStruct((sources, receivers, 2 * F), jnp.float32),
        scratch_shapes=[
            pltpu.VMEM((3, sources * points, F), jnp.float32),
            pltpu.VMEM((3, points * 8, F), jnp.float32),
        ],
        compiler_params=pltpu.CompilerParams(vmem_limit_bytes=VMEM),
    )(left, right)


def gather_and_scatter(src_traces, rec_traces, weight):
    table = fourier_table(src_traces.shape[2])
    left = spectra(src_traces, table)
    right = lax.all_gather(spectra(rec_traces, table), "src", axis=1, tiled=True)
    return lax.psum_scatter(blocks_of(left, right), "xl", scatter_dimension=1, tiled=True) * weight


def swap(value, axis, flip):
    count = lax.axis_size(axis)
    return lax.ppermute(value, axis, [(i, i ^ flip) for i in range(count)])


def side_of(z):
    return (z + 1) // 2 % 2


def cross(value, other):
    return lax.ppermute(value, "src", [(z, z ^ (1 if side_of(z) ^ other else 2)) for z in range(4)])


def deliver(value, op, flip):
    members = lax.axis_size("xl")
    pairs = []
    for z in range(lax.axis_size("src")):
        for chip in range(members // 2):
            for core in range(2):
                tile = z ^ chip ^ TURNS[op][core]
                target = (z ^ (tile & 1)) * members + (z ^ (tile & 2)) * 2 + (core ^ flip)
                pairs.append((z * members + chip * 2 + core, target))
    return lax.ppermute(value, ("src", "xl"), pairs)


def four_planes(src_traces, rec_traces, weight):
    table = fourier_table(src_traces.shape[2])
    z, member = lax.axis_index("src"), lax.axis_index("xl")
    place = [one.reshape(1).astype(jnp.int32) for one in (side_of(z), member % 2, z ^ (member // 2))]
    samples = src_traces.shape[2]
    blocks = src_traces.shape[1] // POINTS
    src_blocks = src_traces.reshape(16, blocks, POINTS, samples)
    rec_blocks = rec_traces.reshape(blocks, 16, POINTS, samples)
    one, far_one, other, far_other = [], [], [], []
    token = None
    for first, count in ONES:
        if token is None:
            token = first_spectra(place[0], count, src_blocks, rec_blocks, table)
        else:
            token = either_spectra(place[0], 0, first, count, src_blocks, rec_blocks, table, token)
        far = cross(token, 0)
        one += [(token, i) for i in range(count)]
        far_one += [(far, i) for i in range(count)]
    for first, count in OTHERS:
        token = either_spectra(place[0], 1, first, count, src_blocks, rec_blocks, table, token)
        far = cross(token, 1)
        other += [(token, i) for i in range(count)]
        far_other += [(far, i) for i in range(count)]
    early = [tiles_of(place, one, [other], after=(token,))]
    sums, after = None, (early[0],)
    for first, count in ONES:
        here = slice(first, first + count)
        sums = tiles_of(place, one[here], [far_one[here]], sums, after)
        after = ()
    early.append(sums)
    sums = None
    for first, count in OTHERS:
        here = slice(first, first + count)
        kept = early if first + count == blocks else ()
        sums = tiles_of(place, far_other[here], [other[here], far_one[here]], sums, (early[1],), kept)
    kept = [*early, sums[0]]
    came = [swap(send, "xl", 1) for send in sums[1:]]
    shape = came[0].shape
    (first,) = pair_of(first_kernel_of_pair, place, kept, came[0], [shape])
    second, third = pair_of(second_kernel_of_pair, place, kept, came[1], [shape[1:]] * 2)
    keep, send = halves_of(place, deliver(first, 0, 0))
    parts = [keep, swap(send, "xl", 1), deliver(second, 1, 0), deliver(third, 1, 1)]
    return sum(part.astype(jnp.float32) for part in parts) * weight


def per_device(src_traces, rec_traces):
    planes, members = lax.axis_size("src"), lax.axis_size("xl")
    weight = float(np.float32(1.0 / math.sqrt(src_traces.shape[1] * members)))
    if planes == 4 and members == 8 and rec_traces.shape[:2] == (4 * POINTS, 16) and src_traces.shape[:2] == (16, 4 * POINTS):
        return four_planes(src_traces, rec_traces, weight)
    return gather_and_scatter(src_traces, rec_traces, weight)


def solution(mesh):
    return jax.shard_map(
        per_device,
        mesh=mesh,
        in_specs=(P("src", "xl", None), P("xl", "src", None)),
        out_specs=P("src", "xl", None),
        check_vma=False,
    )
```

```python
import functools
import math

import jax
import jax.numpy as jnp
import ml_dtypes
import numpy as np
from jax import lax
from jax.experimental import pallas as pl
from jax.experimental.pallas import tpu as pltpu
from jax.sharding import PartitionSpec as P

F = 128
FBASE = 4
VMEM = 40 << 20
POINTS = 8
ROWS = 16 * POINTS
ONES = ((0, 2), (2, 2))
OTHERS = ((0, 2), (2, 1), (3, 1))
TURNS = ((3, 2), (0, 1))


def fourier_table(samples):
    times = np.arange(samples // 2)[:, None]
    bins = FBASE + np.arange(F)
    angles = times * bins[None, :] % samples * (2.0 * math.pi / samples)
    basis = np.concatenate([np.cos(angles), -np.sin(angles)], axis=1)
    basis = (basis / math.sqrt(samples)).astype(np.float32)
    high = basis.astype(ml_dtypes.bfloat16)
    low = (basis - high.astype(np.float32)).astype(ml_dtypes.bfloat16)
    return jnp.asarray(high), jnp.asarray(low)


def transform(traces, high_table, low_table):
    rows, samples = traces.shape
    half = samples // 2
    halves = jnp.concatenate([traces[:, :half], traces[:, half:]], axis=0)
    high = halves.astype(jnp.bfloat16)
    low = (halves - high.astype(jnp.float32)).astype(jnp.bfloat16)
    dot = functools.partial(jnp.dot, preferred_element_type=jnp.float32)
    total = dot(high, high_table) + (dot(high, low_table) + dot(low, high_table))
    odd = (FBASE + lax.broadcasted_iota(jnp.int32, (1, 2 * F), 1)) % 2
    return total[:rows] + total[rows:] * (1 - 2 * odd).astype(jnp.float32)


def spectra_kernel(traces_ref, high_ref, low_ref, out_ref):
    traces = traces_ref[...].reshape(-1, traces_ref.shape[-1])
    total = transform(traces, high_ref[...], low_ref[...])
    out_ref[...] = total.astype(jnp.bfloat16).reshape(out_ref.shape)


def spectra(traces, table):
    rows, width, samples = traces.shape
    block = 8 if rows % 8 == 0 else rows
    whole = pl.BlockSpec((samples // 2, 2 * F), lambda i: (0, 0))
    return pl.pallas_call(
        spectra_kernel,
        grid=(rows // block,),
        in_specs=[pl.BlockSpec((block, width, samples), lambda i: (i, 0, 0)), whole, whole],
        out_specs=pl.BlockSpec((block, width, 2 * F), lambda i: (i, 0, 0)),
        out_shape=jax.ShapeDtypeStruct((rows, width, 2 * F), jnp.bfloat16),
        compiler_params=pltpu.CompilerParams(vmem_limit_bytes=VMEM),
    )(traces, *table)


def first_kernel(side_ref, src_ref, rec_ref, high_ref, low_ref, out_ref, traces, high, low, sems, *, blocks):
    tables = [
        pltpu.make_async_copy(high_ref, high, sems.at[0]),
        pltpu.make_async_copy(low_ref, low, sems.at[1]),
    ]
    choices = [
        [pltpu.make_async_copy(rec_ref.at[i], traces.at[i], sems.at[2 + i]) for i in range(blocks)],
        [pltpu.make_async_copy(src_ref.at[:, i], traces.at[i], sems.at[2 + i]) for i in range(blocks)],
    ]
    for side, copies in enumerate(choices):

        @pl.when(side_ref[0] == side)
        def _(copies=copies):
            for copy in copies:
                copy.start()

    for copy in tables:
        copy.start()
    for side, copies in enumerate(choices):

        @pl.when(side_ref[0] == side)
        def _(copies=copies):
            for copy in copies:
                copy.wait()

    for copy in tables:
        copy.wait()
    total = transform(traces[...].reshape(-1, traces.shape[-1]), high[...], low[...])
    out_ref[...] = total.astype(jnp.bfloat16)


def first_spectra(side, blocks, src_blocks, rec_blocks, table):
    samples = src_blocks.shape[3]
    operands = [pltpu.with_memory_space_constraint(one, pltpu.HBM) for one in (src_blocks, rec_blocks, *table)]
    return pl.pallas_call(
        functools.partial(first_kernel, blocks=blocks),
        in_specs=[pl.BlockSpec(memory_space=pltpu.SMEM)] + [pl.BlockSpec(memory_space=pltpu.HBM)] * 4,
        out_specs=pl.BlockSpec(memory_space=pltpu.VMEM),
        out_shape=jax.ShapeDtypeStruct((blocks * ROWS, 2 * F), jnp.bfloat16),
        scratch_shapes=[
            pltpu.VMEM((blocks, 16, POINTS, samples), jnp.float32),
            pltpu.VMEM((samples // 2, 2 * F), jnp.bfloat16),
            pltpu.VMEM((samples // 2, 2 * F), jnp.bfloat16),
            pltpu.SemaphoreType.DMA((2 + blocks,)),
        ],
        compiler_params=pltpu.CompilerParams(vmem_limit_bytes=VMEM),
    )(side, *operands)


def either_kernel(side_ref, src_ref, rec_ref, high_ref, low_ref, *refs, other, first, blocks):
    out_ref = refs[-1]
    samples = src_ref.shape[-1]
    from_src = (side_ref[0] ^ other) == 1
    parts = []
    for i in range(first, first + blocks):
        src, rec = src_ref[:, i].reshape(ROWS, samples), rec_ref[i].reshape(ROWS, samples)
        parts.append(jnp.where(from_src, src, rec))
    total = transform(jnp.concatenate(parts, axis=0), high_ref[...], low_ref[...])
    out_ref[...] = total.astype(jnp.bfloat16)


def either_spectra(side, other, first, blocks, src_blocks, rec_blocks, table, after):
    samples = src_blocks.shape[3]
    rows = blocks * ROWS
    vmem = pl.BlockSpec(memory_space=pltpu.VMEM)
    return pl.pallas_call(
        functools.partial(either_kernel, other=other, first=first, blocks=blocks),
        in_specs=[pl.BlockSpec(memory_space=pltpu.SMEM)] + [vmem] * 4 + [pl.BlockSpec(memory_space=pl.ANY)],
        out_specs=vmem,
        out_shape=jax.ShapeDtypeStruct((rows, 2 * F), jnp.bfloat16),
        compiler_params=pltpu.CompilerParams(vmem_limit_bytes=VMEM),
        cost_estimate=pl.CostEstimate(
            flops=rows, bytes_accessed=rows, transcendentals=0
        ),
    )(side, src_blocks, rec_blocks, *table, after)


def products(left, right, points, starts, emit):
    many, groups = 4, len(starts)

    def some_sources(block, carry):
        def some_points(step, sums):
            sums = list(sums)
            for inner in range(POINTS):
                point = step * POINTS + inner
                rights = [
                    [right[k, pl.ds(pl.multiple_of(point * 16 + at, 8), 8), :] for at in starts] for k in range(3)
                ]
                for s in range(many):
                    row = (block * many + s) * points + point
                    for k in range(3):
                        one = left[k, pl.ds(row, 1), :]
                        for g in range(groups):
                            i = (s * groups + g) * 3 + k
                            sums[i] = sums[i] + one * rights[k][g]
            return tuple(sums)

        zero = jnp.zeros((8, F), jnp.float32)
        sums = lax.fori_loop(0, points // POINTS, some_points, (zero,) * (many * groups * 3))
        for s in range(many):
            for g in range(groups):
                first, second, third = sums[(s * groups + g) * 3 :][:3]
                emit(block * many + s, g, first - third, first + second)
        return carry

    lax.fori_loop(0, 16 // many, some_sources, 0, unroll=2)


def split(ref, block, forms, at, points, side):
    left = side.astype(jnp.float32)
    right = 1.0 - left

    def some_rows(step, carry):
        value = ref[pl.ds(pl.multiple_of(block * ROWS + step * 16, 16), 16)].astype(jnp.float32)
        for half in range(2):
            re, im = value[half * 8 : half * 8 + 8, :F], value[half * 8 : half * 8 + 8, F:]
            row = step * 2 + half
            start = jnp.where(side == 1, row * points + at * POINTS, at * ROWS + row * 8)
            here = pl.ds(pl.multiple_of(start, 8), 8)
            forms[0, here] = re + im * left
            forms[1, here] = im * right + re * (left - right)
            forms[2, here] = im + re * right
        return carry

    lax.fori_loop(0, ROWS // 16, some_rows, 0, unroll=8)


def tiles_kernel(side_ref, *refs, arrays, ones, others, carried, spare):
    operands, out, forms = refs[:arrays], refs[-2], refs[-1]
    before = refs[arrays] if carried else None
    side = side_ref[0]
    points = len(ones) * POINTS
    for at, (array, block) in enumerate(ones):
        split(operands[array], block, forms.at[0], at, points, side)
    for tile, blocks in enumerate(others):
        for at, (array, block) in enumerate(blocks):
            split(operands[array], block, forms.at[1 + tile], at, points, 1 - side)

    def tile_of(tile, carry):
        left = forms.at[jnp.where(side == 1, 0, 1 + tile)]
        right = forms.at[jnp.where(side == 1, 1 + tile, 0)]

        def emit(source, group, re, im):
            if carried:
                re = re + before[tile, group, source, :, :F]
                im = im + before[tile, group, source, :, F:]
            out[tile, group, source, :, :F] = re
            out[tile, group, source, :, F:] = im

        products(left, right, points, (0, 8), emit)
        return carry

    lax.fori_loop(0, len(others), tile_of, 0)


def tile_at(place, core, op):
    side, _, turn = place
    tile = turn ^ jnp.where(core == 0, *TURNS[op])
    middle = jnp.logical_or(tile == 1, tile == 2)
    return jnp.where(jnp.logical_and(middle, side == 1), 3 - tile, tile)


def with_tile(place, kept, use):
    first = 0
    for array in kept:
        count = array.shape[0]

        @pl.when(jnp.logical_and(place >= first, place < first + count))
        def _(array=array, first=first):
            use(array.at[place - first])

        first += count


def last_tiles_kernel(side_ref, core_ref, turn_ref, *refs, kept, **options):
    place = side_ref[0], core_ref[0], turn_ref[0]
    earlier, sends = refs[:kept], refs[-3:-1]
    refs = refs[kept:-3] + refs[-1:]
    tiles_kernel(side_ref, *refs, **options)
    for op, send in enumerate(sends):

        def use(tile, send=send):
            send[...] = tile[...].astype(send.dtype)

        with_tile(tile_at(place, 1 - place[1], op), [*earlier, refs[-2]], use)


def tiles_of(place, ones, others, before=None, after=(), kept=()):
    arrays = []

    def placed(blocks):
        result = []
        for array, block in blocks:
            if not any(array is one for one in arrays):
                arrays.append(array)
            result.append(([array is one for one in arrays].index(True), block))
        return result

    ones, others = placed(ones), [placed(blocks) for blocks in others]
    count = len(others)
    out_shape = [jax.ShapeDtypeStruct((count, 2, 16, 8, 2 * F), jnp.float32)]
    if kept:
        out_shape += [jax.ShapeDtypeStruct((2, 16, 8, 2 * F), jnp.bfloat16)] * 2
    operands = [*kept, *arrays] + ([] if before is None else [before])
    vmem = pl.BlockSpec(memory_space=pltpu.VMEM)
    options = dict(arrays=len(arrays), ones=ones, others=others, carried=before is not None, spare=len(after))
    kernel = functools.partial(tiles_kernel, **options)
    scalars = place if kept else place[:1]
    if kept:
        kernel = functools.partial(last_tiles_kernel, kept=len(kept), **options)
    result = pl.pallas_call(
        kernel,
        in_specs=[pl.BlockSpec(memory_space=pltpu.SMEM)] * len(scalars)
        + [vmem] * len(operands)
        + [pl.BlockSpec(memory_space=pl.ANY)] * len(after),
        out_specs=[vmem] * len(out_shape),
        out_shape=out_shape,
        scratch_shapes=[pltpu.VMEM((1 + count, 3, len(ones) * ROWS, F), jnp.float32)],
        compiler_params=pltpu.CompilerParams(vmem_limit_bytes=VMEM),
        cost_estimate=pl.CostEstimate(flops=count, bytes_accessed=count, transcendentals=0),
    )(*scalars, *operands, *after)
    return result if kept else result[0]


def first_kernel_of_pair(side_ref, core_ref, turn_ref, *refs, kept):
    place = side_ref[0], core_ref[0], turn_ref[0]
    came, out = refs[kept:]

    def use(tile):
        out[...] = (tile[...] + came[...].astype(jnp.float32)).astype(out.dtype)

    with_tile(tile_at(place, place[1], 0), refs[:kept], use)


def second_kernel_of_pair(side_ref, core_ref, turn_ref, *refs, kept):
    place = side_ref[0], core_ref[0], turn_ref[0]
    came = refs[kept]

    def use(tile):
        for out, half in zip(refs[kept + 1 :], (place[1], 1 - place[1])):
            out[...] = (tile[half] + came[half].astype(jnp.float32)).astype(out.dtype)

    with_tile(tile_at(place, place[1], 1), refs[:kept], use)


def pair_of(kernel, place, kept, came, shapes):
    vmem = pl.BlockSpec(memory_space=pltpu.VMEM)
    return pl.pallas_call(
        functools.partial(kernel, kept=len(kept)),
        in_specs=[pl.BlockSpec(memory_space=pltpu.SMEM)] * 3 + [vmem] * (len(kept) + 1),
        out_specs=[vmem] * len(shapes),
        out_shape=[jax.ShapeDtypeStruct(one, jnp.bfloat16) for one in shapes],
        compiler_params=pltpu.CompilerParams(vmem_limit_bytes=VMEM),
    )(*place, *kept, came)


def halves_kernel(core_ref, whole, keep, send):
    own = core_ref[0]
    keep[...] = whole[own]
    send[...] = whole[1 - own]


def halves_of(place, whole):
    vmem = pl.BlockSpec(memory_space=pltpu.VMEM)
    return pl.pallas_call(
        halves_kernel,
        in_specs=[pl.BlockSpec(memory_space=pltpu.SMEM), vmem],
        out_specs=(vmem, vmem),
        out_shape=(jax.ShapeDtypeStruct(whole.shape[1:], jnp.bfloat16),) * 2,
        compiler_params=pltpu.CompilerParams(vmem_limit_bytes=VMEM),
    )(place[1], whole)


def block_kernel(left_ref, right_ref, out_ref, left_forms, right_forms):
    @pl.when(pl.program_id(0) == 0)
    def _():
        value = left_ref[...].astype(jnp.float32).reshape(-1, 2 * F)
        re, im = value[:, :F], value[:, F:]
        left_forms[0], left_forms[1], left_forms[2] = re + im, re, im

    value = right_ref[...].astype(jnp.float32).reshape(-1, 2 * F)
    re, im = value[:, :F], value[:, F:]
    right_forms[0], right_forms[1], right_forms[2] = re, im - re, re + im
    sources, points, _ = left_ref.shape

    def one_source(source, carry):
        def one_point(point, sums):
            row = source * points + point
            here = pl.ds(pl.multiple_of(point * 8, 8), 8)
            return tuple(total + left_forms[k, pl.ds(row, 1), :] * right_forms[k, here, :] for k, total in enumerate(sums))

        zero = jnp.zeros((8, F), jnp.float32)
        first, second, third = lax.fori_loop(0, points, one_point, (zero,) * 3)
        out_ref[source, :, :F] = first - third
        out_ref[source, :, F:] = first + second
        return carry

    lax.fori_loop(0, sources, one_source, 0)


def blocks_of(left, right):
    sources, points, _ = left.shape
    receivers = right.shape[1]
    return pl.pallas_call(
        block_kernel,
        grid=(receivers // 8,),
        in_specs=[
            pl.BlockSpec((sources, points, 2 * F), lambda i: (0, 0, 0)),
            pl.BlockSpec((points, 8, 2 * F), lambda i: (0, i, 0)),
        ],
        out_specs=pl.BlockSpec((sources, 8, 2 * F), lambda i: (0, i, 0)),
        out_shape=jax.ShapeDtypeStruct((sources, receivers, 2 * F), jnp.float32),
        scratch_shapes=[
            pltpu.VMEM((3, sources * points, F), jnp.float32),
            pltpu.VMEM((3, points * 8, F), jnp.float32),
        ],
        compiler_params=pltpu.CompilerParams(vmem_limit_bytes=VMEM),
    )(left, right)


def gather_and_scatter(src_traces, rec_traces, weight):
    table = fourier_table(src_traces.shape[2])
    left = spectra(src_traces, table)
    right = lax.all_gather(spectra(rec_traces, table), "src", axis=1, tiled=True)
    return lax.psum_scatter(blocks_of(left, right), "xl", scatter_dimension=1, tiled=True) * weight


def swap(value, axis, flip):
    count = lax.axis_size(axis)
    return lax.ppermute(value, axis, [(i, i ^ flip) for i in range(count)])


def side_of(z):
    return (z + 1) // 2 % 2


def cross(value, other):
    return lax.ppermute(value, "src", [(z, z ^ (1 if side_of(z) ^ other else 2)) for z in range(4)])


def deliver(value, op, flip):
    members = lax.axis_size("xl")
    pairs = []
    for z in range(lax.axis_size("src")):
        for chip in range(members // 2):
            for core in range(2):
                tile = z ^ chip ^ TURNS[op][core]
                target = (z ^ (tile & 1)) * members + (z ^ (tile & 2)) * 2 + (core ^ flip)
                pairs.append((z * members + chip * 2 + core, target))
    return lax.ppermute(value, ("src", "xl"), pairs)


def four_planes(src_traces, rec_traces, weight):
    table = fourier_table(src_traces.shape[2])
    z, member = lax.axis_index("src"), lax.axis_index("xl")
    place = [one.reshape(1).astype(jnp.int32) for one in (side_of(z), member % 2, z ^ (member // 2))]
    samples = src_traces.shape[2]
    blocks = src_traces.shape[1] // POINTS
    src_blocks = src_traces.reshape(16, blocks, POINTS, samples)
    rec_blocks = rec_traces.reshape(blocks, 16, POINTS, samples)
    one, far_one, other, far_other = [], [], [], []
    token = None
    for first, count in ONES:
        if token is None:
            token = first_spectra(place[0], count, src_blocks, rec_blocks, table)
        else:
            token = either_spectra(place[0], 0, first, count, src_blocks, rec_blocks, table, token)
        far = cross(token, 0)
        one += [(token, i) for i in range(count)]
        far_one += [(far, i) for i in range(count)]
    for first, count in OTHERS:
        token = either_spectra(place[0], 1, first, count, src_blocks, rec_blocks, table, token)
        far = cross(token, 1)
        other += [(token, i) for i in range(count)]
        far_other += [(far, i) for i in range(count)]
    sums, after = None, (token,)
    for first, count in ONES:
        here = slice(first, first + count)
        sums = tiles_of(place, one[here], [far_one[here]], sums, after)
        after = ()
    early = [tiles_of(place, one, [other], after=(sums,)), sums]
    sums = None
    for first, count in OTHERS:
        here = slice(first, first + count)
        kept = early if first + count == blocks else ()
        sums = tiles_of(place, far_other[here], [other[here], far_one[here]], sums, (early[0],), kept)
    kept = [*early, sums[0]]
    came = [swap(send, "xl", 1) for send in sums[1:]]
    shape = came[0].shape
    (first,) = pair_of(first_kernel_of_pair, place, kept, came[0], [shape])
    second, third = pair_of(second_kernel_of_pair, place, kept, came[1], [shape[1:]] * 2)
    keep, send = halves_of(place, deliver(first, 0, 0))
    parts = [keep, swap(send, "xl", 1), deliver(second, 1, 0), deliver(third, 1, 1)]
    return sum(part.astype(jnp.float32) for part in parts) * weight


def per_device(src_traces, rec_traces):
    planes, members = lax.axis_size("src"), lax.axis_size("xl")
    weight = float(np.float32(1.0 / math.sqrt(src_traces.shape[1] * members)))
    if planes == 4 and members == 8 and rec_traces.shape[:2] == (4 * POINTS, 16) and src_traces.shape[:2] == (16, 4 * POINTS):
        return four_planes(src_traces, rec_traces, weight)
    return gather_and_scatter(src_traces, rec_traces, weight)


def solution(mesh):
    return jax.shard_map(
        per_device,
        mesh=mesh,
        in_specs=(P("src", "xl", None), P("xl", "src", None)),
        out_specs=P("src", "xl", None),
        check_vma=False,
    )
```
